32 devices in a mesh: seq: 8 (over z, y), grp: 4 (over x, core).
Axes of the slice: x: 2, y: 2, z: 4, core: 2. Of those that a mesh axis runs over, the one named last changes fastest.
Arguments:
- x_group: bfloat16 [2048, 2304], P('seq'), may hold values from -6 to 6
- decode_input: bfloat16 [3, 64, 2304], P(None, 'seq'), may hold values from -6 to 6
- prompt_len: int32 [64], P('seq'), may hold values from 1 to 768, as said below
- latent_pages: bfloat16 [8, 8, 12, 64, 576], P('seq'), may hold values from -6 to 6
- slot_target: int32 [8, 8, 12], P(None, 'seq'), may hold values from 0 to 95, as said below
- page_counts: int32 [8, 8], P(None, 'seq'), may hold values from 0 to 12, as said below
- kda_state: float32 [64, 32, 128, 128], P(None, 'grp', 'seq'), may hold values from -4 to 4
- query_proj: bfloat16 [2304, 6144], P(None, 'grp'), may hold values from -1 to 1
- latent_proj: bfloat16 [2304, 576], replicated, may hold values from -1 to 1
- key_expand: bfloat16 [512, 4096], P(None, 'grp'), may hold values from -1 to 1
- value_expand: bfloat16 [512, 4096], P(None, 'grp'), may hold values from -0.25 to 0.25
- mla_output: bfloat16 [4096, 2304], P('grp'), may hold values from -0.09375 to 0.09375
- kda_inputs: bfloat16 [2304, 3, 4096], P(None, None, 'grp'), may hold values from -0.125 to 0.125
- kda_beta: bfloat16 [2304, 32], P(None, 'grp'), may hold values from -0.125 to 0.125
- decay_down: bfloat16 [2304, 128], replicated, may hold values from -0.125 to 0.125
- decay_up: bfloat16 [128, 4096], P(None, 'grp'), may hold values from -0.5 to 0.5
- gate_down: bfloat16 [2304, 128], replicated, may hold values from -0.125 to 0.125
- gate_up: bfloat16 [128, 4096], P(None, 'grp'), may hold values from -0.5 to 0.5
- decay_log: float32 [32], P('grp'), may hold values from -2.5 to 0.5
- kda_output: bfloat16 [4096, 2304], P('grp'), may hold values from -0.09375 to 0.09375
Outputs:
- prefill_out: bfloat16 [2048, 2304], P('seq', 'grp')
- decode_out: bfloat16 [3, 64, 2304], P(None, 'seq', 'grp')
The draws below stay inside these ranges and needn't reach their ends.
Inputs may be any that keep to these rules, and one draw needn't show every extreme that they name: A request has ceil(prompt_len / 64) pages, at most 12; on one owner drawn from the seed all 8 requests have 12 pages. `slot_target`: entry k < page_counts[s, d] holds local request * 12 + page of owner d; every page of every request is held in exactly one slot; entries past the count are 0. `page_counts`: slots are filled from slot 0; the count 12 is reached on some pair in every draw.
All inputs are finite; a program needn't handle non-finite values.
Results may differ from the reference program's by a relative error of at most 0.02.
Values may be sent and summed in bfloat16 or wider, within the bound.
A program may use at most 192 MiB of HBM per device.

```python
import jax
import jax.numpy as jnp
from jax import lax

D = 2304
HEADS = 32
LAT = 512
ROPE = 64
NOPE = 128
VH = 128
KH = 32
DK = 128
DV = 128
REQ_DEV = 8
PAGE = 64
MAXP = 12
STEPS = 3
GROUP = 2048
REQUESTS = 64
CAP = 12
N_SEQ = 8


def handoff_plan(key):
    subkeys = jax.random.split(key, 4)
    owner_of = jnp.arange(REQUESTS) // REQ_DEV
    page_number = jax.random.randint(subkeys[0], (REQUESTS,), 1, MAXP + 1)
    fullest = jax.random.randint(subkeys[1], (), 0, N_SEQ)
    page_number = jnp.where(owner_of == fullest, MAXP, page_number)
    tails = jax.random.randint(subkeys[2], (REQUESTS,), 1, PAGE + 1)
    lengths = (page_number - 1) * PAGE + tails
    grid_pages = page_number.reshape(N_SEQ, REQ_DEV)
    starts = jnp.cumsum(grid_pages, axis=1) - grid_pages
    page_index = jnp.arange(MAXP)
    ordinal = starts[:, :, None] + page_index[None, None, :]
    valid = page_index[None, None, :] < grid_pages[:, :, None]
    orders = jax.vmap(lambda single: jax.random.permutation(single, N_SEQ))(jax.random.split(subkeys[3], N_SEQ))
    source = jnp.take_along_axis(orders, (ordinal % N_SEQ).reshape(N_SEQ, -1), axis=1).reshape(ordinal.shape)
    source = jnp.where(valid, source, N_SEQ)
    slot = ordinal // N_SEQ
    target = jnp.broadcast_to(jnp.arange(REQ_DEV)[None, :, None] * MAXP + page_index[None, None, :], ordinal.shape)
    owner = jnp.broadcast_to(jnp.arange(N_SEQ)[:, None, None], ordinal.shape)
    slot_target = jnp.zeros((N_SEQ, N_SEQ, CAP), jnp.int32).at[source, owner, slot].set(target.astype(jnp.int32), mode='drop')
    page_counts = jnp.zeros((N_SEQ, N_SEQ), jnp.int32).at[source, owner].add(jnp.ones(ordinal.shape, jnp.int32), mode='drop')
    return (lengths.astype(jnp.int32), slot_target, page_counts)


def draw_prompt_len(key, part):
    return handoff_plan(key)[0]


def draw_slot_target(key, part):
    return handoff_plan(key)[1]


def draw_page_counts(key, part):
    return handoff_plan(key)[2]


def draw_x_group(key, part):
    key = jax.random.fold_in(key, 21)
    shape = (GROUP, D)
    values = jnp.clip(jax.random.normal(key, shape), -6.0, 6.0)
    return values.astype(jnp.bfloat16)


def draw_decode_input(key, part):
    key = jax.random.fold_in(key, 22)
    shape = (STEPS, REQUESTS, D)
    values = jnp.clip(jax.random.normal(key, shape), -6.0, 6.0)
    return values.astype(jnp.bfloat16)


def draw_latent_pages(key, part):
    key = jax.random.fold_in(key, 23)
    shape = (N_SEQ, N_SEQ, CAP, PAGE, LAT + ROPE)
    values = jnp.clip(jax.random.normal(key, shape), -6.0, 6.0)
    return values.astype(jnp.bfloat16)


def draw_query_proj(key, part):
    key = jax.random.fold_in(key, 24)
    head_width = NOPE + ROPE
    values = jnp.clip(jax.random.normal(key, (D, HEADS, head_width)), -4.0, 4.0) * D ** (-0.5)
    return values.reshape(D, HEADS * head_width).astype(jnp.bfloat16)


def draw_latent_proj(key, part):
    key = jax.random.fold_in(key, 25)
    values = jnp.clip(jax.random.normal(key, (D, LAT + ROPE)), -4.0, 4.0) * D ** (-0.5)
    return values.astype(jnp.bfloat16)


def draw_key_expand(key, part):
    key = jax.random.fold_in(key, 26)
    values = jnp.clip(jax.random.normal(key, (LAT, HEADS, NOPE)), -4.0, 4.0) * LAT ** (-0.5)
    return values.reshape(LAT, HEADS * NOPE).astype(jnp.bfloat16)


def steps_of(rng, shape, cuts, smallest, largest):
    def one(axis_at, shards_of):
        steps = jax.random.uniform(jax.random.fold_in(jax.random.fold_in(rng, 6), axis_at), (shards_of,), jnp.float32, smallest / len(cuts), largest / len(cuts))
        return jnp.repeat(jnp.exp(steps), shape[axis_at] // shards_of).reshape((-1,) + (1,) * (len(shape) - axis_at - 1))

    loudness = one(*cuts[0])
    for cut in cuts[1:]:
        loudness = loudness * one(*cut)
    return loudness


def noise(own_key, extent, spread, limit, cuts=(), held_as=jnp.bfloat16):
    factor_of = steps_of(own_key, extent, cuts, -0.22, 0.18) if cuts else 1.0
    drawn = jax.random.normal(own_key, extent, jnp.float32) * spread * factor_of
    return jnp.minimum(jnp.maximum(drawn, -limit), limit).astype(held_as)


def setup_inputs(seed: int = 0) -> dict:
    key_of = jax.random.split(jax.random.key(seed), 21)
    return {
        "x_group": draw_x_group(jax.random.fold_in(key_of[20], 71), 0),
        "decode_input": draw_decode_input(jax.random.fold_in(key_of[20], 71), 0),
        "prompt_len": draw_prompt_len(jax.random.fold_in(key_of[20], 71), 0),
        "latent_pages": draw_latent_pages(jax.random.fold_in(key_of[20], 71), 0),
        "slot_target": draw_slot_target(jax.random.fold_in(key_of[20], 71), 0),
        "page_counts": draw_page_counts(jax.random.fold_in(key_of[20], 71), 0),
        "kda_state": noise(key_of[6], (REQUESTS, KH, DV, DK), 0.5, 4.0, ((1, 4), (2, 8)), jnp.float32),
        "query_proj": draw_query_proj(jax.random.fold_in(key_of[20], 71), 0),
        "latent_proj": draw_latent_proj(jax.random.fold_in(key_of[20], 71), 0),
        "key_expand": draw_key_expand(jax.random.fold_in(key_of[20], 71), 0),
        "value_expand": noise(key_of[10], (LAT, HEADS * VH), LAT ** -0.5, 0.25, ((1, 4),)),
        "mla_output": noise(key_of[11], (HEADS * VH, D), (HEADS * VH) ** -0.5, 0.09375, ((0, 4),)),
        "kda_inputs": noise(key_of[12], (D, 3, KH * DK), D ** -0.5, 0.125, ((2, 4),)),
        "kda_beta": noise(key_of[13], (D, KH), D ** -0.5, 0.125, ((1, 4),)),
        "decay_down": noise(key_of[14], (D, DK), D ** -0.5, 0.125),
        "decay_up": noise(key_of[15], (DK, KH * DK), DK ** -0.5, 0.5, ((1, 4),)),
        "gate_down": noise(key_of[16], (D, DK), D ** -0.5, 0.125),
        "gate_up": noise(key_of[17], (DK, KH * DV), DK ** -0.5, 0.5, ((1, 4),)),
        "decay_log": jnp.clip(-2.5 + 3.0 * jax.random.uniform(key_of[18], (KH,), jnp.float32) ** steps_of(key_of[18], (KH,), ((0, 4),), -0.2, 0.2), -2.5, 0.5),
        "kda_output": noise(key_of[19], (KH * DV, D), (KH * DV) ** -0.5, 0.09375, ((0, 4),)),
    }


epsilon = 1e-06
masked_score = -1e+30

def norm_rows(values):
    return values * lax.rsqrt(lax.optimization_barrier(jnp.mean(values * values, axis=-1, keepdims=True)) + epsilon)

def unit_rows(values):
    return values * lax.rsqrt(lax.optimization_barrier(jnp.sum(values * values, axis=-1, keepdims=True)) + epsilon)

def rotate(values, position):
    halfway = values.shape[-1] // 2
    frequency = jnp.exp(-jnp.log(10000.0) * jnp.arange(halfway, dtype=jnp.float32) / halfway)
    angles = position.astype(jnp.float32)[..., None] * frequency
    leading = values[..., :halfway]
    trailing = values[..., halfway:]
    return jnp.concatenate([leading * jnp.cos(angles) - trailing * jnp.sin(angles), leading * jnp.sin(angles) + trailing * jnp.cos(angles)], axis=-1)

def make_latent(normed, latent_proj, position):
    projected = jnp.dot(normed, latent_proj, preferred_element_type=jnp.float32)
    return jnp.concatenate([norm_rows(projected[:, :LAT]), rotate(projected[:, LAT:], position)], axis=-1).astype(jnp.bfloat16)

def make_query(normed, query_proj, position):
    head_count = query_proj.shape[1] // (NOPE + ROPE)
    projected = jnp.dot(normed, query_proj, preferred_element_type=jnp.float32).reshape(normed.shape[0], head_count, NOPE + ROPE)
    return (projected[..., :NOPE].astype(jnp.bfloat16), rotate(projected[..., NOPE:], position[:, None]).astype(jnp.bfloat16))

def absorb(q_nope, q_rope, key_expand):
    head_count = q_nope.shape[1]
    latent_query = jnp.einsum('rhn,chn->rhc', q_nope.astype(jnp.float32), key_expand.reshape(LAT, head_count, NOPE).astype(jnp.float32))
    return jnp.concatenate([latent_query.astype(jnp.bfloat16), q_rope], axis=-1)

def partial_attend(queries, key_rows, live_mask):
    scores = jnp.einsum('rhc,kc->rhk', queries.astype(jnp.float32), key_rows.astype(jnp.float32)) * (NOPE + ROPE) ** (-0.5)
    scores = jnp.where(live_mask[:, None, :], scores, masked_score)
    highest = lax.optimization_barrier(jnp.max(scores, axis=-1))
    weights = jnp.where(live_mask[:, None, :], jnp.exp(scores - highest[..., None]), 0.0)
    totals = lax.optimization_barrier(jnp.sum(weights, axis=-1))
    summed = jnp.einsum('rhk,kc->rhc', weights.astype(jnp.bfloat16).astype(jnp.float32), key_rows[:, :LAT].astype(jnp.float32))
    return (highest, totals, summed)

def cache_mask(target, counts, lengths, offset, width):
    slot_live = jnp.arange(target.shape[1])[None, :] < counts[:, None]
    request = target // MAXP
    token_pos = (target % MAXP)[..., None] * PAGE + offset + jnp.arange(width)[None, None, :]
    owners = jnp.arange(lengths.shape[0])[:, None, None, None]
    live = slot_live[None, :, :, None] & (request[None, :, :, None] == owners) & (token_pos[None] < lengths[:, None, None, None])
    return live.reshape(lengths.shape[0], -1)

def prefill(x_group, query_proj, latent_proj, key_expand, value_expand, mla_output):
    rows_in = x_group.astype(jnp.float32)
    normed = norm_rows(rows_in).astype(jnp.bfloat16)
    group_rows = x_group.shape[0]
    position = jnp.arange(group_rows)
    q_nope, q_rope = make_query(normed, query_proj, position)
    latent = make_latent(normed, latent_proj, position)
    k_nope = jnp.dot(latent[:, :LAT], key_expand, preferred_element_type=jnp.float32).astype(jnp.bfloat16).reshape(group_rows, HEADS, NOPE)
    values = jnp.dot(latent[:, :LAT], value_expand, preferred_element_type=jnp.float32).astype(jnp.bfloat16).reshape(group_rows, HEADS, VH)
    causal = position[None, :] <= position[:, None]
    rope_keys = latent[:, LAT:]

    def one_head(inputs):
        head_nope, head_rope, head_keys, head_values = inputs
        scores = (jnp.dot(head_nope, head_keys.T, preferred_element_type=jnp.float32) + jnp.dot(head_rope, rope_keys.T, preferred_element_type=jnp.float32)) * (NOPE + ROPE) ** (-0.5)
        scores = jnp.where(causal, scores, masked_score)
        highest = lax.optimization_barrier(jnp.max(scores, axis=-1))
        weights = jnp.where(causal, jnp.exp(scores - highest[:, None]), 0.0)
        totals = lax.optimization_barrier(jnp.sum(weights, axis=-1))
        summed = jnp.dot(weights.astype(jnp.bfloat16), head_values, preferred_element_type=jnp.float32)
        return (summed / totals[:, None]).astype(jnp.bfloat16)
    heads_out = lax.map(one_head, (q_nope.transpose(1, 0, 2), q_rope.transpose(1, 0, 2), k_nope.transpose(1, 0, 2), values.transpose(1, 0, 2)))
    flat = heads_out.transpose(1, 0, 2).reshape(group_rows, HEADS * VH)
    return (rows_in + jnp.dot(flat, mla_output, preferred_element_type=jnp.float32)).astype(jnp.bfloat16)

def reference(x_group, decode_input, prompt_len, latent_pages, slot_target, page_counts, kda_state, query_proj, latent_proj, key_expand, value_expand, mla_output, kda_inputs, kda_beta, decay_down, decay_up, gate_down, gate_up, decay_log, kda_output):
    prefill_out = prefill(x_group, query_proj, latent_proj, key_expand, value_expand, mla_output)
    rows_in = decode_input.astype(jnp.float32)
    dec_normed = norm_rows(rows_in).astype(jnp.bfloat16)
    query_list = []
    fresh_list = []
    for step_index in range(STEPS):
        place = prompt_len + step_index
        q_nope, q_rope = make_query(dec_normed[step_index], query_proj, place)
        query_list.append(absorb(q_nope, q_rope, key_expand))
        fresh_list.append(make_latent(dec_normed[step_index], latent_proj, place))
    queries = jnp.stack(query_list).reshape(STEPS, N_SEQ, REQ_DEV, HEADS, LAT + ROPE).transpose(1, 0, 2, 3, 4)
    fresh_all = jnp.stack(fresh_list).reshape(STEPS, N_SEQ, REQ_DEV, LAT + ROPE).transpose(1, 0, 2, 3)
    cache_all = latent_pages.transpose(1, 0, 2, 3, 4).reshape(N_SEQ, N_SEQ * CAP * PAGE, LAT + ROPE)

    def owner_attend(inputs):
        key_rows, target, counts, lengths, owner_queries, fresh_keys = inputs
        live = cache_mask(target, counts, lengths, 0, PAGE)
        results = []
        for step_index in range(STEPS):
            new_keys = fresh_keys[:step_index + 1].reshape(-1, LAT + ROPE)
            new_live = (jnp.arange(new_keys.shape[0]) % REQ_DEV)[None, :] == jnp.arange(REQ_DEV)[:, None]
            highest, totals, summed = partial_attend(owner_queries[step_index], jnp.concatenate([key_rows, new_keys], axis=0), jnp.concatenate([live, new_live], axis=1))
            results.append((summed / totals[..., None]).astype(jnp.bfloat16))
        return jnp.stack(results)
    latent_outs = lax.map(owner_attend, (cache_all, slot_target.transpose(1, 0, 2), page_counts.T, prompt_len.reshape(N_SEQ, REQ_DEV), queries, fresh_all))
    latent_outs = latent_outs.transpose(1, 0, 2, 3, 4).reshape(STEPS, REQUESTS, HEADS, LAT)
    states = kda_state.astype(jnp.float32)
    outputs = []
    for step_index in range(STEPS):
        head_values = jnp.einsum('rhc,chv->rhv', latent_outs[step_index].astype(jnp.float32), value_expand.reshape(LAT, HEADS, VH).astype(jnp.float32)).astype(jnp.bfloat16)
        hidden = rows_in[step_index] + jnp.dot(head_values.reshape(REQUESTS, HEADS * VH), mla_output, preferred_element_type=jnp.float32)
        kda_in = norm_rows(hidden).astype(jnp.bfloat16)
        projected = jnp.dot(kda_in, kda_inputs.reshape(D, 3 * KH * DK), preferred_element_type=jnp.float32).reshape(REQUESTS, 3, KH, DK)
        queries_kda = unit_rows(projected[:, 0]) * DK ** (-0.5)
        keys_kda = unit_rows(projected[:, 1])
        values_kda = projected[:, 2]
        write_rate = jax.nn.sigmoid(jnp.dot(kda_in, kda_beta, preferred_element_type=jnp.float32))
        decay_low = jnp.dot(kda_in, decay_down, preferred_element_type=jnp.float32).astype(jnp.bfloat16)
        decays = jnp.exp(-jnp.exp(decay_log)[None, :, None] * jax.nn.softplus(jnp.dot(decay_low, decay_up, preferred_element_type=jnp.float32).reshape(REQUESTS, KH, DK)))
        gate_low = jnp.dot(kda_in, gate_down, preferred_element_type=jnp.float32).astype(jnp.bfloat16)
        out_gate = jax.nn.sigmoid(jnp.dot(gate_low, gate_up, preferred_element_type=jnp.float32).reshape(REQUESTS, KH, DV))
        states = states * decays[:, :, None, :]
        errors = values_kda - lax.optimization_barrier(jnp.sum(states * keys_kda[:, :, None, :], axis=-1))
        states = states + write_rate[..., None, None] * errors[..., None] * keys_kda[:, :, None, :]
        readout = lax.optimization_barrier(jnp.sum(states * queries_kda[:, :, None, :], axis=-1))
        blended = (norm_rows(readout) * out_gate).astype(jnp.bfloat16).reshape(REQUESTS, KH * DV)
        outputs.append((hidden + jnp.dot(blended, kda_output, preferred_element_type=jnp.float32)).astype(jnp.bfloat16))
    return (prefill_out, jnp.stack(outputs))
```

```python
import jax
import jax.numpy as jnp
from jax import lax
from jax.experimental import pallas as pl
from jax.experimental.pallas import tpu as pltpu
from jax.sharding import PartitionSpec as P

LAT = 512
ROPE = 64
NOPE = 128
VH = 128
DK = 128
DV = 128
PAGE = 64
MAXP = 12


epsilon = 1e-06
masked_score = -1e30


def norm_rows(values):
    return values * lax.rsqrt(jnp.mean(values * values, axis=-1, keepdims=True) + epsilon)


def unit_rows(values):
    return values * lax.rsqrt(jnp.sum(values * values, axis=-1, keepdims=True) + epsilon)


def rotate(values, position):
    halfway = values.shape[-1] // 2
    frequency = jnp.exp(-jnp.log(10000.0) * jnp.arange(halfway, dtype=jnp.float32) / halfway)
    angles = position.astype(jnp.float32)[..., None] * frequency
    leading = values[..., :halfway]
    trailing = values[..., halfway:]
    return jnp.concatenate(
        [
            leading * jnp.cos(angles) - trailing * jnp.sin(angles),
            leading * jnp.sin(angles) + trailing * jnp.cos(angles),
        ],
        axis=-1,
    )


def make_latent(normed, latent_proj, position):
    projected = jnp.dot(normed, latent_proj, preferred_element_type=jnp.float32)
    return jnp.concatenate(
        [norm_rows(projected[:, :LAT]), rotate(projected[:, LAT:], position)], axis=-1
    ).astype(jnp.bfloat16)


def make_query(normed, query_proj, position):
    head_count = query_proj.shape[1] // (NOPE + ROPE)
    projected = jnp.dot(normed, query_proj, preferred_element_type=jnp.float32).reshape(
        normed.shape[0], head_count, NOPE + ROPE
    )
    return (
        projected[..., :NOPE].astype(jnp.bfloat16),
        rotate(projected[..., NOPE:], position[:, None]).astype(jnp.bfloat16),
    )


def prefill_body(place_ref, query_ref, rows_ref, key_ref, value_ref, out_ref, peak, total, mixed):
    pair, group_rows, _ = query_ref.shape
    nt = (((1,), (1,)), ((), ()))
    factor = (NOPE + ROPE) ** (-0.5) * 1.4426950408889634
    own = place_ref[0]

    def chunk(index, first):
        rows = rows_ref[pl.ds(pl.multiple_of(index * group_rows, group_rows), group_rows), :]
        latent = rows[:, :LAT]
        keys = jnp.dot(latent, key_ref[...], preferred_element_type=jnp.float32)
        keys = keys.astype(jnp.bfloat16)
        values = lax.dot_general(value_ref[...], latent, nt, preferred_element_type=jnp.float32)
        values = values.astype(jnp.bfloat16)
        for h in range(pair):
            full = jnp.concatenate([keys[:, h * NOPE : (h + 1) * NOPE], rows[:, LAT:]], axis=1)
            scores = lax.dot_general(full, query_ref[h], nt, preferred_element_type=jnp.float32)
            if first:
                key_at = lax.broadcasted_iota(jnp.int32, scores.shape, 0)
                query_at = lax.broadcasted_iota(jnp.int32, scores.shape, 1)
                scores = jnp.where(key_at <= query_at, scores, masked_score)
            top = jnp.max(scores, axis=0, keepdims=True)
            if not first:
                top = jnp.maximum(top, peak[h])
            weights = jnp.exp2((scores - top) * factor)
            summed = jnp.sum(weights, axis=0, keepdims=True)
            added = jnp.dot(
                values[h * VH : (h + 1) * VH],
                weights.astype(jnp.bfloat16),
                preferred_element_type=jnp.float32,
            )
            if first:
                total[h] = summed
                mixed[h] = added
            else:
                shrink = jnp.exp2((peak[h] - top) * factor)
                total[h] = total[h] * shrink + summed
                mixed[h] = mixed[h] * shrink + added
            peak[h] = top

    chunk(own, True)

    @pl.loop(0, own)
    def _(index):
        chunk(index, False)

    for h in range(pair):
        out_ref[:, h * VH : (h + 1) * VH] = (mixed[h] / total[h]).T.astype(out_ref.dtype)


def prefill_attend(seq_index, queries, rows, key_expand, value_expand):
    heads, group_rows, _ = queries.shape
    pair = 2
    row_count = rows.shape[0]
    return pl.pallas_call(
        prefill_body,
        out_shape=jax.ShapeDtypeStruct((group_rows, heads * VH), jnp.bfloat16),
        grid_spec=pltpu.PrefetchScalarGridSpec(
            num_scalar_prefetch=1,
            grid=(heads // pair,),
            in_specs=[
                pl.BlockSpec((pair, group_rows, NOPE + ROPE), lambda h, p: (h, 0, 0)),
                pl.BlockSpec((row_count, LAT + ROPE), lambda h, p: (0, 0)),
                pl.BlockSpec((LAT, pair * NOPE), lambda h, p: (0, h)),
                pl.BlockSpec((pair * VH, LAT), lambda h, p: (h, 0)),
            ],
            out_specs=pl.BlockSpec((group_rows, pair * VH), lambda h, p: (0, h)),
            scratch_shapes=[
                pltpu.VMEM((pair, 1, group_rows), jnp.float32),
                pltpu.VMEM((pair, 1, group_rows), jnp.float32),
                pltpu.VMEM((pair, VH, group_rows), jnp.float32),
            ],
        ),
        compiler_params=pltpu.CompilerParams(vmem_limit_bytes=40 * 1024 * 1024),
        cost_estimate=pl.CostEstimate(
            flops=2 * heads * group_rows * row_count * 4 * NOPE,
            bytes_accessed=row_count * (LAT + ROPE) * 4,
            transcendentals=heads * group_rows * row_count,
        ),
        name="prefill_attend",
    )(seq_index.reshape(1).astype(jnp.int32), queries, rows, key_expand, value_expand.T)


def shards(
    x_group,
    decode_input,
    prompt_len,
    latent_pages,
    slot_target,
    page_counts,
    kda_state,
    query_proj,
    latent_proj,
    key_expand,
    value_expand,
    mla_output,
    kda_inputs,
    kda_beta,
    decay_down,
    decay_up,
    gate_down,
    gate_up,
    decay_log,
    kda_output,
):
    f32, bf16 = jnp.float32, jnp.bfloat16
    seq_index = lax.axis_index("seq")
    grp_index = lax.axis_index("grp")
    owners = lax.axis_size("seq")
    heads = key_expand.shape[1] // NOPE
    kheads = decay_log.shape[0]
    width = x_group.shape[1]
    share = width // lax.axis_size("grp")
    col = grp_index * share
    scale = (NOPE + ROPE) ** (-0.5)
    steps, reqs, _ = decode_input.shape
    cap = slot_target.shape[2]
    n = steps * reqs

    dec_own = decode_input.reshape(n, width)
    dec_all = lax.all_gather(dec_own, "seq", axis=0, tiled=True)
    ints = jnp.concatenate([prompt_len, page_counts[:, 0], slot_target.reshape(-1)])
    ints = lax.all_gather(ints, "seq", axis=0)
    lens_all = ints[:, :reqs]
    counts = lax.dynamic_slice_in_dim(ints, reqs + seq_index, 1, 1)
    targets = lax.dynamic_slice_in_dim(ints, reqs + owners + seq_index * cap, cap, 1)

    states = lax.all_to_all(
        kda_state.astype(bf16), "seq", split_axis=0, concat_axis=2, tiled=True
    )

    group_rows = x_group.shape[0]
    rows_share = group_rows // lax.axis_size("grp")
    x_normed = norm_rows(x_group.astype(f32)).astype(bf16)
    own_normed = norm_rows(dec_own.astype(f32)).astype(bf16)
    own_place = (prompt_len[None, :] + jnp.arange(steps)[:, None]).reshape(n)
    share_normed = lax.dynamic_slice_in_dim(x_normed, grp_index * rows_share, rows_share, 0)
    share_place = seq_index * group_rows + grp_index * rows_share + jnp.arange(rows_share)
    latents = make_latent(
        jnp.concatenate([share_normed, own_normed]),
        latent_proj,
        jnp.concatenate([share_place, own_place]),
    )
    fresh = latents[rows_share:]
    shard_rows = lax.all_gather(latents[:rows_share], ("seq", "grp"), axis=0, tiled=True)

    dec_normed = norm_rows(dec_all.astype(f32)).astype(bf16)
    dec_place = (lens_all[:, None, :] + jnp.arange(steps)[None, :, None]).reshape(owners * n)
    dq_nope, dq_rope = make_query(dec_normed, query_proj, dec_place)
    latent_query = jnp.einsum(
        "rhn,chn->rhc", dq_nope, key_expand.reshape(LAT, heads, NOPE), preferred_element_type=f32
    ).astype(bf16)
    qc = jnp.concatenate([latent_query, dq_rope], axis=-1).reshape(owners, n * heads, LAT + ROPE)
    pages = latent_pages.reshape(owners, cap * PAGE, LAT + ROPE)
    slot_live = jnp.arange(cap)[None, :] < counts
    token = (targets % MAXP)[..., None] * PAGE + jnp.arange(PAGE)
    live = (
        slot_live[:, None, :, None]
        & ((targets // MAXP)[:, None, :, None] == jnp.arange(reqs)[None, :, None, None])
        & (token[:, None] < lens_all[:, :, None, None])
    ).reshape(owners, 1, reqs, 1, cap * PAGE)
    scores = jnp.einsum("oqc,okc->oqk", qc, pages, preferred_element_type=f32) * scale
    scores = scores.reshape(owners, steps, reqs, heads, cap * PAGE)
    scores = jnp.where(live, scores, masked_score)
    highest = jnp.max(scores, axis=-1, keepdims=True)
    weights = jnp.where(live, jnp.exp(scores - highest), 0.0)
    totals = jnp.sum(weights, axis=-1)
    summed = jnp.einsum(
        "oqk,okc->oqc",
        weights.astype(bf16).reshape(owners, n * heads, cap * PAGE),
        pages[:, :, :LAT],
        preferred_element_type=f32,
    ).reshape(owners * n, heads, LAT)
    safe = jnp.maximum(totals, 1e-30)
    part = (summed / safe.reshape(owners * n, heads, 1)).astype(bf16)
    part = jnp.einsum(
        "rhc,chv->rhv", part, value_expand.reshape(LAT, heads, VH), preferred_element_type=f32
    ).astype(bf16)
    lse = jnp.where(totals > 0, highest[..., 0] + jnp.log(safe), masked_score).reshape(
        owners, n, heads
    )
    lse_hi = lax.reduce_precision(lse, 8, 7)
    lse_lo = lse - lse_hi
    sent = jnp.concatenate(
        [part.reshape(owners, n, heads * VH), lse_hi.astype(bf16), lse_lo.astype(bf16)], axis=-1
    )
    came = lax.all_to_all(sent, "seq", split_axis=0, concat_axis=0, tiled=True)

    position = seq_index * group_rows + jnp.arange(group_rows)
    q_nope, q_rope = make_query(x_normed, query_proj, position)
    queries = jnp.concatenate([q_nope, q_rope], axis=-1).transpose(1, 0, 2)
    heads_out = prefill_attend(seq_index, queries, shard_rows, key_expand, value_expand)
    prefill_part = jnp.dot(heads_out, mla_output, preferred_element_type=f32)
    attended = lax.psum_scatter(
        prefill_part.astype(bf16), "grp", scatter_dimension=1, tiled=True
    ).astype(f32)
    prefill_out = (
        lax.dynamic_slice_in_dim(x_group, col, share, 1).astype(f32) + attended
    ).astype(bf16)

    own_nope = lax.dynamic_slice_in_dim(dq_nope, seq_index * n, n, 0)
    own_rope = lax.dynamic_slice_in_dim(dq_rope, seq_index * n, n, 0)
    fresh_k = jnp.dot(fresh[:, :LAT], key_expand, preferred_element_type=f32).astype(bf16)
    fresh_v = jnp.dot(fresh[:, :LAT], value_expand, preferred_element_type=f32).astype(bf16)
    fresh_scores = (
        jnp.einsum(
            "qhn,khn->hqk", own_nope, fresh_k.reshape(n, heads, NOPE), preferred_element_type=f32
        )
        + jnp.einsum("qhr,kr->hqk", own_rope, fresh[:, LAT:], preferred_element_type=f32)
    ) * scale
    at = jnp.arange(n)
    fresh_live = (
        (at[:, None] % reqs == at[None, :] % reqs) & (at[None, :] // reqs <= at[:, None] // reqs)
    )[None]
    fresh_scores = jnp.where(fresh_live, fresh_scores, masked_score)
    lse_came = came[..., heads * VH :].astype(f32)
    lse_came = (lse_came[..., :heads] + lse_came[..., heads:]).transpose(0, 2, 1)
    top = jnp.maximum(jnp.max(fresh_scores, axis=-1), jnp.max(lse_came, axis=0))
    fresh_w = jnp.where(fresh_live, jnp.exp(fresh_scores - top[..., None]), 0.0)
    came_w = jnp.exp(lse_came - top[None])
    total = jnp.sum(fresh_w, axis=-1) + jnp.sum(came_w, axis=0)
    mixed = jnp.einsum(
        "hqk,khv->qhv",
        fresh_w.astype(bf16),
        fresh_v.reshape(n, heads, VH),
        preferred_element_type=f32,
    )
    parts = came[..., : heads * VH].astype(f32).reshape(owners, n, heads, VH)
    mixed = mixed + jnp.sum(parts * came_w.transpose(0, 2, 1)[..., None], axis=0)
    head_values = (mixed / total.T[..., None]).astype(bf16).reshape(n, heads * VH)
    mla_part = jnp.dot(head_values, mla_output, preferred_element_type=f32)
    hidden = dec_own.astype(f32) + lax.psum(mla_part.astype(bf16), "grp").astype(f32)

    kda_in = norm_rows(hidden).astype(bf16)
    projected = jnp.dot(
        kda_in, kda_inputs.reshape(width, -1), preferred_element_type=f32
    ).reshape(n, 3, kheads, DK)
    split = (steps, reqs, kheads, DK)
    queries_kda = (unit_rows(projected[:, 0]) * DK ** (-0.5)).reshape(split)
    keys_kda = unit_rows(projected[:, 1]).reshape(split)
    values_kda = projected[:, 2].reshape(split)
    beta = jax.nn.sigmoid(jnp.dot(kda_in, kda_beta, preferred_element_type=f32))
    beta = beta.reshape(steps, reqs, kheads, 1)
    decay_low = jnp.dot(kda_in, decay_down, preferred_element_type=f32).astype(bf16)
    decays = jnp.exp(
        -jnp.exp(decay_log)[None, :, None]
        * jax.nn.softplus(
            jnp.dot(decay_low, decay_up, preferred_element_type=f32).reshape(n, kheads, DK)
        )
    ).reshape(split)
    gate_low = jnp.dot(kda_in, gate_down, preferred_element_type=f32).astype(bf16)
    out_gate = jax.nn.sigmoid(
        jnp.dot(gate_low, gate_up, preferred_element_type=f32).reshape(n, kheads, DV)
    )
    decayed = decays[0]
    looks = []
    for t in range(steps):
        if t:
            decayed = decayed * decays[t]
        looks += [keys_kda[t] * decayed, queries_kda[t] * decayed]
    seen = jnp.einsum(
        "rhxk,rhvk->rhxv",
        jnp.stack(looks, axis=2).astype(bf16),
        states,
        preferred_element_type=f32,
    )
    written = []
    reads = []
    for t in range(steps):
        if t:
            written = [(e, k * decays[t]) for e, k in written]
        err = values_kda[t] - seen[:, :, 2 * t]
        for e, k in written:
            err = err - e * jnp.sum(k * keys_kda[t], axis=-1, keepdims=True)
        written.append((beta[t] * err, keys_kda[t]))
        read = seen[:, :, 2 * t + 1]
        for e, k in written:
            read = read + e * jnp.sum(k * queries_kda[t], axis=-1, keepdims=True)
        reads.append(read)
    readout = jnp.stack(reads).reshape(n, kheads, DV)
    blended = (norm_rows(readout) * out_gate).astype(bf16).reshape(n, kheads * DV)
    kda_part = jnp.dot(blended, kda_output, preferred_element_type=f32)
    kda_share = lax.psum_scatter(
        kda_part.astype(bf16), "grp", scatter_dimension=1, tiled=True
    ).astype(f32)
    decode_out = (lax.dynamic_slice_in_dim(hidden, col, share, 1) + kda_share).astype(bf16)
    return (prefill_out, decode_out.reshape(steps, reqs, share))


def solution(mesh):
    in_specs = (
        P("seq", None),
        P(None, "seq", None),
        P("seq"),
        P("seq", None, None, None, None),
        P(None, "seq", None),
        P(None, "seq"),
        P(None, "grp", "seq", None),
        P(None, "grp"),
        P(),
        P(None, "grp"),
        P(None, "grp"),
        P("grp", None),
        P(None, None, "grp"),
        P(None, "grp"),
        P(),
        P(None, "grp"),
        P(),
        P(None, "grp"),
        P("grp"),
        P("grp", None),
    )
    out_specs = (P("seq", "grp"), P(None, "seq", "grp"))
    return jax.shard_map(shards, mesh=mesh, in_specs=in_specs, out_specs=out_specs, check_vma=False)
```

```python
import functools

import jax
import jax.numpy as jnp
from jax import lax
from jax.experimental import pallas as pl
from jax.experimental.pallas import tpu as pltpu
from jax.sharding import PartitionSpec as P

LAT = 512
ROPE = 64
NOPE = 128
VH = 128
DK = 128
DV = 128
PAGE = 64
MAXP = 12


epsilon = 1e-06
masked_score = -1e30


def norm_rows(values):
    return values * lax.rsqrt(jnp.mean(values * values, axis=-1, keepdims=True) + epsilon)


def unit_rows(values):
    return values * lax.rsqrt(jnp.sum(values * values, axis=-1, keepdims=True) + epsilon)


def rotate(values, position):
    halfway = values.shape[-1] // 2
    frequency = jnp.exp(-jnp.log(10000.0) * jnp.arange(halfway, dtype=jnp.float32) / halfway)
    angles = position.astype(jnp.float32)[..., None] * frequency
    leading = values[..., :halfway]
    trailing = values[..., halfway:]
    return jnp.concatenate(
        [
            leading * jnp.cos(angles) - trailing * jnp.sin(angles),
            leading * jnp.sin(angles) + trailing * jnp.cos(angles),
        ],
        axis=-1,
    )


def make_latent(normed, latent_proj, position):
    projected = jnp.dot(normed, latent_proj, preferred_element_type=jnp.float32)
    return jnp.concatenate(
        [norm_rows(projected[:, :LAT]), rotate(projected[:, LAT:], position)], axis=-1
    ).astype(jnp.bfloat16)


def make_query(normed, query_proj, position):
    head_count = query_proj.shape[1] // (NOPE + ROPE)
    projected = jnp.dot(normed, query_proj, preferred_element_type=jnp.float32).reshape(
        normed.shape[0], head_count, NOPE + ROPE
    )
    return (
        projected[..., :NOPE].astype(jnp.bfloat16),
        rotate(projected[..., NOPE:], position[:, None]).astype(jnp.bfloat16),
    )


def prefill_body(place_ref, query_ref, rows_ref, key_ref, value_ref, out_ref, peak, total, mixed):
    pair, group_rows, _ = query_ref.shape
    nt = (((1,), (1,)), ((), ()))
    factor = (NOPE + ROPE) ** (-0.5) * 1.4426950408889634
    own = place_ref[0]

    def chunk(index, first):
        rows = rows_ref[pl.ds(pl.multiple_of(index * group_rows, group_rows), group_rows), :]
        latent = rows[:, :LAT]
        keys = jnp.dot(latent, key_ref[...], preferred_element_type=jnp.float32)
        keys = keys.astype(jnp.bfloat16)
        values = lax.dot_general(value_ref[...], latent, nt, preferred_element_type=jnp.float32)
        values = values.astype(jnp.bfloat16)
        for h in range(pair):
            full = jnp.concatenate([keys[:, h * NOPE : (h + 1) * NOPE], rows[:, LAT:]], axis=1)
            scores = lax.dot_general(full, query_ref[h], nt, preferred_element_type=jnp.float32)
            if first:
                key_at = lax.broadcasted_iota(jnp.int32, scores.shape, 0)
                query_at = lax.broadcasted_iota(jnp.int32, scores.shape, 1)
                scores = jnp.where(key_at <= query_at, scores, masked_score)
            top = jnp.max(scores, axis=0, keepdims=True)
            if not first:
                top = jnp.maximum(top, peak[h])
            weights = jnp.exp2((scores - top) * factor)
            summed = jnp.sum(weights, axis=0, keepdims=True)
            added = jnp.dot(
                values[h * VH : (h + 1) * VH],
                weights.astype(jnp.bfloat16),
                preferred_element_type=jnp.float32,
            )
            if first:
                total[h] = summed
                mixed[h] = added
            else:
                shrink = jnp.exp2((peak[h] - top) * factor)
                total[h] = total[h] * shrink + summed
                mixed[h] = mixed[h] * shrink + added
            peak[h] = top

    chunk(own, True)

    @pl.loop(0, own)
    def _(index):
        chunk(index, False)

    for h in range(pair):
        out_ref[:, h * VH : (h + 1) * VH] = (mixed[h] / total[h]).T.astype(out_ref.dtype)


def prefill_attend(seq_index, queries, rows, key_expand, value_expand):
    heads, group_rows, _ = queries.shape
    pair = 2
    row_count = rows.shape[0]
    return pl.pallas_call(
        prefill_body,
        out_shape=jax.ShapeDtypeStruct((group_rows, heads * VH), jnp.bfloat16),
        grid_spec=pltpu.PrefetchScalarGridSpec(
            num_scalar_prefetch=1,
            grid=(heads // pair,),
            in_specs=[
                pl.BlockSpec((pair, group_rows, NOPE + ROPE), lambda h, p: (h, 0, 0)),
                pl.BlockSpec((row_count, LAT + ROPE), lambda h, p: (0, 0)),
                pl.BlockSpec((LAT, pair * NOPE), lambda h, p: (0, h)),
                pl.BlockSpec((pair * VH, LAT), lambda h, p: (h, 0)),
            ],
            out_specs=pl.BlockSpec((group_rows, pair * VH), lambda h, p: (0, h)),
            scratch_shapes=[
                pltpu.VMEM((pair, 1, group_rows), jnp.float32),
                pltpu.VMEM((pair, 1, group_rows), jnp.float32),
                pltpu.VMEM((pair, VH, group_rows), jnp.float32),
            ],
        ),
        compiler_params=pltpu.CompilerParams(vmem_limit_bytes=40 * 1024 * 1024),
        cost_estimate=pl.CostEstimate(
            flops=2 * heads * group_rows * row_count * 4 * NOPE,
            bytes_accessed=row_count * (LAT + ROPE) * 4,
            transcendentals=heads * group_rows * row_count,
        ),
        name="prefill_attend",
    )(seq_index.reshape(1).astype(jnp.int32), queries, rows, key_expand, value_expand.T)


def gather_body(owners, own_ref, all_ref, send_sem, recv_sem, local_sem):
    me = lax.axis_index("seq")
    rows = own_ref.shape[0]
    barrier = pltpu.get_barrier_semaphore()
    for step in range(1, owners):
        peer = lax.rem(me + step, owners)
        pl.semaphore_signal(
            barrier, inc=1, device_id={"seq": peer}, device_id_type=pl.DeviceIdType.MESH
        )
    pl.semaphore_wait(barrier, owners - 1)
    place = all_ref.at[pl.ds(pl.multiple_of(me * rows, rows), rows)]
    copies = []
    for step in range(1, owners):
        peer = lax.rem(me + step, owners)
        copies.append(
            pltpu.make_async_remote_copy(
                src_ref=own_ref,
                dst_ref=place,
                send_sem=send_sem.at[step],
                recv_sem=recv_sem.at[step],
                device_id={"seq": peer},
                device_id_type=pl.DeviceIdType.MESH,
            )
        )
        copies[-1].start()
    local = pltpu.make_async_copy(own_ref, place, local_sem)
    local.start()
    local.wait()
    for copy in copies:
        copy.wait()


def gather_rows(own, owners):
    rows, width = own.shape
    return pl.pallas_call(
        functools.partial(gather_body, owners),
        out_shape=jax.ShapeDtypeStruct((owners * rows, width), own.dtype),
        in_specs=[pl.BlockSpec(memory_space=pltpu.VMEM)],
        out_specs=pl.BlockSpec(memory_space=pltpu.VMEM),
        scratch_shapes=[
            pltpu.SemaphoreType.DMA((owners,)),
            pltpu.SemaphoreType.DMA((owners,)),
            pltpu.SemaphoreType.DMA,
        ],
        compiler_params=pltpu.CompilerParams(collective_id=0, has_side_effects=True),
        name="gather_rows",
    )(own)


def query_body(rows_ref, weight_ref, key_ref, cos_ref, sin_ref, prefill_ref, decode_ref):
    pair, group_rows, _ = prefill_ref.shape
    owners, slab, _ = decode_ref.shape
    each = slab // pair
    nt = (((1,), (1,)), ((), ()))
    projected = jnp.dot(rows_ref[...], weight_ref[...], preferred_element_type=jnp.float32)
    for h in range(pair):
        start = h * (NOPE + ROPE)
        nope = projected[:, start : start + NOPE].astype(jnp.bfloat16)
        rope = projected[:, start + NOPE : start + NOPE + ROPE]
        turned = jnp.concatenate([rope[:, ROPE // 2 :], rope[:, : ROPE // 2]], axis=1)
        rope = (rope * cos_ref[...] + turned * sin_ref[...]).astype(jnp.bfloat16)
        prefill_ref[h] = jnp.concatenate([nope[:group_rows], rope[:group_rows]], axis=1)
        latent = lax.dot_general(
            nope[group_rows:],
            key_ref[:, h * NOPE : (h + 1) * NOPE],
            nt,
            preferred_element_type=jnp.float32,
        ).astype(jnp.bfloat16)
        full = jnp.concatenate([latent, rope[group_rows:]], axis=1)
        decode_ref[:, h * each : (h + 1) * each, :] = full.reshape(owners, each, LAT + ROPE)


def make_queries(rows, group_rows, owners, query_proj, key_expand, cosine, sine):
    pair = 2
    total, width = rows.shape
    heads = key_expand.shape[1] // NOPE
    each = (total - group_rows) // owners
    return pl.pallas_call(
        query_body,
        out_shape=(
            jax.ShapeDtypeStruct((heads, group_rows, NOPE + ROPE), jnp.bfloat16),
            jax.ShapeDtypeStruct((owners, heads * each, LAT + ROPE), jnp.bfloat16),
        ),
        grid=(heads // pair,),
        in_specs=[
            pl.BlockSpec((total, width), lambda h: (0, 0)),
            pl.BlockSpec((width, pair * (NOPE + ROPE)), lambda h: (0, h)),
            pl.BlockSpec((LAT, pair * NOPE), lambda h: (0, h)),
            pl.BlockSpec((total, ROPE), lambda h: (0, 0)),
            pl.BlockSpec((total, ROPE), lambda h: (0, 0)),
        ],
        out_specs=(
            pl.BlockSpec((pair, group_rows, NOPE + ROPE), lambda h: (h, 0, 0)),
            pl.BlockSpec((owners, pair * each, LAT + ROPE), lambda h: (0, h, 0)),
        ),
        compiler_params=pltpu.CompilerParams(vmem_limit_bytes=40 * 1024 * 1024),
        cost_estimate=pl.CostEstimate(
            flops=2 * total * width * query_proj.shape[1],
            bytes_accessed=2 * width * (query_proj.shape[1] + total),
            transcendentals=0,
        ),
        name="make_queries",
    )(rows, query_proj, key_expand, cosine, sine)


def page_body(reqs, query_ref, page_ref, holder_ref, value_ref, out_ref, parts, logs):
    owner = pl.program_id(0)
    heads, _, _ = parts.shape
    rows = query_ref.shape[1]
    each = rows // heads
    keys = page_ref[0]
    nt = (((1,), (1,)), ((), ()))
    scores = lax.dot_general(query_ref[0], keys, nt, preferred_element_type=jnp.float32)
    request = lax.rem(lax.broadcasted_iota(jnp.int32, (rows, 1), 0), reqs)
    live = holder_ref[0] == request
    scores = jnp.where(live, scores * (NOPE + ROPE) ** (-0.5), masked_score)
    highest = jnp.max(scores, axis=1, keepdims=True)
    weights = jnp.where(live, jnp.exp(scores - highest), 0.0)
    totals = jnp.sum(weights, axis=1, keepdims=True)
    safe = jnp.maximum(totals, 1e-30)
    summed = jnp.dot(weights.astype(jnp.bfloat16), keys[:, :LAT], preferred_element_type=jnp.float32)
    summed = (summed / safe).astype(jnp.bfloat16)
    place = pl.ds(pl.multiple_of(owner * each, each), each)
    parts[:, place, :] = summed.reshape(heads, each, LAT)
    log = jnp.where(totals > 0, highest + jnp.log(safe), masked_score)
    logs[:, place, :] = log.reshape(heads, each, 1)

    @pl.when(owner == pl.num_programs(0) - 1)
    def _():
        lane = lax.broadcasted_iota(jnp.int32, (parts.shape[1], 128), 1)
        tail = jnp.zeros((parts.shape[1], 128), jnp.float32)
        for h in range(heads):
            out_ref[:, h * VH : (h + 1) * VH] = jnp.dot(
                parts[h], value_ref[:, h * VH : (h + 1) * VH], preferred_element_type=jnp.float32
            ).astype(out_ref.dtype)
            high = logs[h].astype(jnp.bfloat16).astype(jnp.float32)
            tail = jnp.where(lane == h, high, tail)
            tail = jnp.where(lane == heads + h, logs[h] - high, tail)
        out_ref[:, heads * VH :] = tail.astype(out_ref.dtype)


def attend_pages(reqs, queries, pages, holders, value_expand):
    owners, rows, depth = queries.shape
    heads = value_expand.shape[1] // VH
    keys = pages.shape[1]
    total = owners * rows // heads
    return pl.pallas_call(
        functools.partial(page_body, reqs),
        out_shape=jax.ShapeDtypeStruct((total, heads * VH + 128), jnp.bfloat16),
        grid=(owners,),
        in_specs=[
            pl.BlockSpec((1, rows, depth), lambda o: (o, 0, 0)),
            pl.BlockSpec((1, keys, depth), lambda o: (o, 0, 0)),
            pl.BlockSpec((1, 1, keys), lambda o: (o, 0, 0)),
            pl.BlockSpec(value_expand.shape, lambda o: (0, 0)),
        ],
        out_specs=pl.BlockSpec((total, heads * VH + 128), lambda o: (0, 0)),
        scratch_shapes=[
            pltpu.VMEM((heads, total, LAT), jnp.bfloat16),
            pltpu.VMEM((heads, total, 1), jnp.float32),
        ],
        compiler_params=pltpu.CompilerParams(vmem_limit_bytes=40 * 1024 * 1024),
        cost_estimate=pl.CostEstimate(
            flops=4 * owners * rows * keys * depth,
            bytes_accessed=2 * owners * keys * depth,
            transcendentals=owners * rows * keys,
        ),
        name="attend_pages",
    )(queries, pages, holders, value_expand)


def shards(
    x_group,
    decode_input,
    prompt_len,
    latent_pages,
    slot_target,
    page_counts,
    kda_state,
    query_proj,
    latent_proj,
    key_expand,
    value_expand,
    mla_output,
    kda_inputs,
    kda_beta,
    decay_down,
    decay_up,
    gate_down,
    gate_up,
    decay_log,
    kda_output,
):
    f32, bf16 = jnp.float32, jnp.bfloat16
    seq_index = lax.axis_index("seq")
    grp_index = lax.axis_index("grp")
    owners = lax.axis_size("seq")
    heads = key_expand.shape[1] // NOPE
    kheads = decay_log.shape[0]
    width = x_group.shape[1]
    share = width // lax.axis_size("grp")
    col = grp_index * share
    scale = (NOPE + ROPE) ** (-0.5)
    steps, reqs, _ = decode_input.shape
    cap = slot_target.shape[2]
    n = steps * reqs

    dec_own = decode_input.reshape(n, width)
    group_rows = x_group.shape[0]
    rows_share = group_rows // lax.axis_size("grp")
    x_normed = norm_rows(x_group.astype(f32)).astype(bf16)
    own_normed = norm_rows(dec_own.astype(f32)).astype(bf16)
    own_place = (prompt_len[None, :] + jnp.arange(steps)[:, None]).reshape(n)
    share_normed = lax.dynamic_slice_in_dim(x_normed, grp_index * rows_share, rows_share, 0)
    share_place = seq_index * group_rows + grp_index * rows_share + jnp.arange(rows_share)
    latents = make_latent(
        jnp.concatenate([share_normed, own_normed]),
        latent_proj,
        jnp.concatenate([share_place, own_place]),
    )
    fresh = latents[rows_share:]
    shard_rows = lax.all_gather(latents[:rows_share], ("seq", "grp"), axis=0, tiled=True)

    each = -(-(n + 1) // 16) * 16
    numbers = jnp.concatenate(
        [prompt_len // PAGE, prompt_len % PAGE, page_counts[:, 0], slot_target.reshape(-1)]
    ).astype(bf16)
    numbers = jnp.pad(numbers, (0, width - numbers.shape[0]))[None]
    payload = jnp.concatenate(
        [own_normed, numbers, jnp.zeros((each - n - 1, width), bf16)], axis=0
    )
    payload, latents = lax.optimization_barrier((payload, latents))
    dec_all = gather_rows(payload, owners)
    numbers = dec_all.reshape(owners, each, width)[:, n, : 2 * reqs + owners + owners * cap]
    ints = numbers.astype(jnp.int32)
    lens_all = ints[:, :reqs] * PAGE + ints[:, reqs : 2 * reqs]
    counts = lax.dynamic_slice_in_dim(ints, 2 * reqs + seq_index, 1, 1)
    targets = lax.dynamic_slice_in_dim(ints, 2 * reqs + owners + seq_index * cap, cap, 1)

    states = lax.all_to_all(
        kda_state.astype(bf16), "seq", split_axis=0, concat_axis=2, tiled=True
    )

    position = seq_index * group_rows + jnp.arange(group_rows)
    dec_place = (lens_all[:, None, :] + jnp.arange(each // reqs)[None, :, None]).reshape(-1)
    place = jnp.concatenate([position, dec_place]).astype(f32)
    half = ROPE // 2
    angles = place[:, None] * jnp.exp(-jnp.log(10000.0) * jnp.arange(half, dtype=f32) / half)
    cosine, sine = jnp.cos(angles), jnp.sin(angles)
    queries, qc = make_queries(
        jnp.concatenate([x_normed, dec_all]),
        group_rows,
        owners,
        query_proj,
        key_expand,
        jnp.concatenate([cosine, cosine], axis=1),
        jnp.concatenate([-sine, sine], axis=1),
    )

    pages = latent_pages.reshape(owners, cap * PAGE, LAT + ROPE)
    token = (targets % MAXP)[..., None] * PAGE + jnp.arange(PAGE)
    holder = targets // MAXP
    length = jnp.sum(
        jnp.where(holder[..., None] == jnp.arange(reqs), lens_all[:, None, :], 0), axis=-1
    )
    live = (jnp.arange(cap)[None, :] < counts)[..., None] & (token < length[..., None])
    holders = jnp.where(live, holder[..., None], -1).reshape(owners, 1, cap * PAGE)
    sent = attend_pages(reqs, qc, pages, holders, value_expand)
    sent, shard_rows = lax.optimization_barrier((sent, shard_rows))
    came = lax.all_to_all(
        sent.reshape(owners, each, -1), "seq", split_axis=0, concat_axis=0, tiled=True
    )

    heads_out = prefill_attend(seq_index, queries, shard_rows, key_expand, value_expand)
    prefill_part = jnp.dot(heads_out, mla_output, preferred_element_type=f32)
    came, prefill_part = lax.optimization_barrier((came, prefill_part))
    attended = lax.psum_scatter(
        prefill_part.astype(bf16), "grp", scatter_dimension=1, tiled=True
    ).astype(f32)
    prefill_out = (
        lax.dynamic_slice_in_dim(x_group, col, share, 1).astype(f32) + attended
    ).astype(bf16)

    came = came[:, :n]
    own_query = lax.dynamic_index_in_dim(qc, seq_index, 0, keepdims=False)
    own_query = own_query.reshape(heads, each, LAT + ROPE)[:, :n]
    fresh_v = jnp.dot(fresh[:, :LAT], value_expand, preferred_element_type=f32).astype(bf16)
    fresh_scores = jnp.einsum("hqc,kc->hqk", own_query, fresh, preferred_element_type=f32) * scale
    at = jnp.arange(n)
    fresh_live = (
        (at[:, None] % reqs == at[None, :] % reqs) & (at[None, :] // reqs <= at[:, None] // reqs)
    )[None]
    fresh_scores = jnp.where(fresh_live, fresh_scores, masked_score)
    lse_came = came[..., heads * VH :].astype(f32)[..., : 2 * heads]
    lse_came = (lse_came[..., :heads] + lse_came[..., heads:]).transpose(0, 2, 1)
    top = jnp.maximum(jnp.max(fresh_scores, axis=-1), jnp.max(lse_came, axis=0))
    fresh_w = jnp.where(fresh_live, jnp.exp(fresh_scores - top[..., None]), 0.0)
    came_w = jnp.exp(lse_came - top[None])
    total = jnp.sum(fresh_w, axis=-1) + jnp.sum(came_w, axis=0)
    mixed = jnp.einsum(
        "hqk,khv->qhv",
        fresh_w.astype(bf16),
        fresh_v.reshape(n, heads, VH),
        preferred_element_type=f32,
    )
    parts = came[..., : heads * VH].astype(f32).reshape(owners, n, heads, VH)
    mixed = mixed + jnp.sum(parts * came_w.transpose(0, 2, 1)[..., None], axis=0)
    head_values = (mixed / total.T[..., None]).astype(bf16).reshape(n, heads * VH)
    mla_part = jnp.dot(head_values, mla_output, preferred_element_type=f32)
    hidden = dec_own.astype(f32) + lax.psum(mla_part.astype(bf16), "grp").astype(f32)

    kda_in = norm_rows(hidden).astype(bf16)
    projected = jnp.dot(
        kda_in, kda_inputs.reshape(width, -1), preferred_element_type=f32
    ).reshape(n, 3, kheads, DK)
    split = (steps, reqs, kheads, DK)
    queries_kda = (unit_rows(projected[:, 0]) * DK ** (-0.5)).reshape(split)
    keys_kda = unit_rows(projected[:, 1]).reshape(split)
    values_kda = projected[:, 2].reshape(split)
    beta = jax.nn.sigmoid(jnp.dot(kda_in, kda_beta, preferred_element_type=f32))
    beta = beta.reshape(steps, reqs, kheads, 1)
    decay_low = jnp.dot(kda_in, decay_down, preferred_element_type=f32).astype(bf16)
    decays = jnp.exp(
        -jnp.exp(decay_log)[None, :, None]
        * jax.nn.softplus(
            jnp.dot(decay_low, decay_up, preferred_element_type=f32).reshape(n, kheads, DK)
        )
    ).reshape(split)
    gate_low = jnp.dot(kda_in, gate_down, preferred_element_type=f32).astype(bf16)
    out_gate = jax.nn.sigmoid(
        jnp.dot(gate_low, gate_up, preferred_element_type=f32).reshape(n, kheads, DV)
    )
    decayed = decays[0]
    looks = []
    for t in range(steps):
        if t:
            decayed = decayed * decays[t]
        looks += [keys_kda[t] * decayed, queries_kda[t] * decayed]
    seen = jnp.einsum(
        "rhxk,rhvk->rhxv",
        jnp.stack(looks, axis=2).astype(bf16),
        states,
        preferred_element_type=f32,
    )
    written = []
    reads = []
    for t in range(steps):
        if t:
            written = [(e, k * decays[t]) for e, k in written]
        err = values_kda[t] - seen[:, :, 2 * t]
        for e, k in written:
            err = err - e * jnp.sum(k * keys_kda[t], axis=-1, keepdims=True)
        written.append((beta[t] * err, keys_kda[t]))
        read = seen[:, :, 2 * t + 1]
        for e, k in written:
            read = read + e * jnp.sum(k * queries_kda[t], axis=-1, keepdims=True)
        reads.append(read)
    readout = jnp.stack(reads).reshape(n, kheads, DV)
    blended = (norm_rows(readout) * out_gate).astype(bf16).reshape(n, kheads * DV)
    kda_part = jnp.dot(blended, kda_output, preferred_element_type=f32)
    kda_share = lax.psum_scatter(
        kda_part.astype(bf16), "grp", scatter_dimension=1, tiled=True
    ).astype(f32)
    decode_out = (lax.dynamic_slice_in_dim(hidden, col, share, 1) + kda_share).astype(bf16)
    return (prefill_out, decode_out.reshape(steps, reqs, share))


def solution(mesh):
    in_specs = (
        P("seq", None),
        P(None, "seq", None),
        P("seq"),
        P("seq", None, None, None, None),
        P(None, "seq", None),
        P(None, "seq"),
        P(None, "grp", "seq", None),
        P(None, "grp"),
        P(),
        P(None, "grp"),
        P(None, "grp"),
        P("grp", None),
        P(None, None, "grp"),
        P(None, "grp"),
        P(),
        P(None, "grp"),
        P(),
        P(None, "grp"),
        P("grp"),
        P("grp", None),
    )
    out_specs = (P("seq", "grp"), P(None, "seq", "grp"))
    return jax.shard_map(shards, mesh=mesh, in_specs=in_specs, out_specs=out_specs, check_vma=False)
```

```python
import functools

import jax
import jax.numpy as jnp
from jax import lax
from jax.experimental import pallas as pl
from jax.experimental.pallas import tpu as pltpu
from jax.sharding import PartitionSpec as P

LAT = 512
ROPE = 64
NOPE = 128
VH = 128
DK = 128
DV = 128
PAGE = 64
MAXP = 12


epsilon = 1e-06
masked_score = -1e30


def norm_rows(values):
    return values * lax.rsqrt(jnp.mean(values * values, axis=-1, keepdims=True) + epsilon)


def unit_rows(values):
    return values * lax.rsqrt(jnp.sum(values * values, axis=-1, keepdims=True) + epsilon)


def rotate(values, position):
    halfway = values.shape[-1] // 2
    frequency = jnp.exp(-jnp.log(10000.0) * jnp.arange(halfway, dtype=jnp.float32) / halfway)
    angles = position.astype(jnp.float32)[..., None] * frequency
    leading = values[..., :halfway]
    trailing = values[..., halfway:]
    return jnp.concatenate(
        [
            leading * jnp.cos(angles) - trailing * jnp.sin(angles),
            leading * jnp.sin(angles) + trailing * jnp.cos(angles),
        ],
        axis=-1,
    )


def make_latent(normed, latent_proj, position):
    projected = jnp.dot(normed, latent_proj, preferred_element_type=jnp.float32)
    return jnp.concatenate(
        [norm_rows(projected[:, :LAT]), rotate(projected[:, LAT:], position)], axis=-1
    ).astype(jnp.bfloat16)


def make_query(normed, query_proj, position):
    head_count = query_proj.shape[1] // (NOPE + ROPE)
    projected = jnp.dot(normed, query_proj, preferred_element_type=jnp.float32).reshape(
        normed.shape[0], head_count, NOPE + ROPE
    )
    return (
        projected[..., :NOPE].astype(jnp.bfloat16),
        rotate(projected[..., NOPE:], position[:, None]).astype(jnp.bfloat16),
    )


def prefill_body(place_ref, query_ref, rows_ref, key_ref, value_ref, out_ref, peak, total, mixed):
    pair, group_rows, _ = query_ref.shape
    nt = (((1,), (1,)), ((), ()))
    factor = (NOPE + ROPE) ** (-0.5) * 1.4426950408889634
    own = place_ref[0]

    def chunk(index, first):
        rows = rows_ref[pl.ds(pl.multiple_of(index * group_rows, group_rows), group_rows), :]
        latent = rows[:, :LAT]
        keys = jnp.dot(latent, key_ref[...], preferred_element_type=jnp.float32)
        keys = keys.astype(jnp.bfloat16)
        values = lax.dot_general(value_ref[...], latent, nt, preferred_element_type=jnp.float32)
        values = values.astype(jnp.bfloat16)
        for h in range(pair):
            full = jnp.concatenate([keys[:, h * NOPE : (h + 1) * NOPE], rows[:, LAT:]], axis=1)
            scores = lax.dot_general(full, query_ref[h], nt, preferred_element_type=jnp.float32)
            if first:
                key_at = lax.broadcasted_iota(jnp.int32, scores.shape, 0)
                query_at = lax.broadcasted_iota(jnp.int32, scores.shape, 1)
                scores = jnp.where(key_at <= query_at, scores, masked_score)
            top = jnp.max(scores, axis=0, keepdims=True)
            if not first:
                top = jnp.maximum(top, peak[h])
            weights = jnp.exp2((scores - top) * factor)
            summed = jnp.sum(weights, axis=0, keepdims=True)
            added = jnp.dot(
                values[h * VH : (h + 1) * VH],
                weights.astype(jnp.bfloat16),
                preferred_element_type=jnp.float32,
            )
            if first:
                total[h] = summed
                mixed[h] = added
            else:
                shrink = jnp.exp2((peak[h] - top) * factor)
                total[h] = total[h] * shrink + summed
                mixed[h] = mixed[h] * shrink + added
            peak[h] = top

    chunk(own, True)

    @pl.loop(0, own)
    def _(index):
        chunk(index, False)

    for h in range(pair):
        out_ref[:, h * VH : (h + 1) * VH] = (mixed[h] / total[h]).T.astype(out_ref.dtype)


def prefill_attend(seq_index, queries, rows, key_expand, value_expand):
    heads, group_rows, _ = queries.shape
    pair = 2
    row_count = rows.shape[0]
    return pl.pallas_call(
        prefill_body,
        out_shape=jax.ShapeDtypeStruct((group_rows, heads * VH), jnp.bfloat16),
        grid_spec=pltpu.PrefetchScalarGridSpec(
            num_scalar_prefetch=1,
            grid=(heads // pair,),
            in_specs=[
                pl.BlockSpec((pair, group_rows, NOPE + ROPE), lambda h, p: (h, 0, 0)),
                pl.BlockSpec((row_count, LAT + ROPE), lambda h, p: (0, 0)),
                pl.BlockSpec((LAT, pair * NOPE), lambda h, p: (0, h)),
                pl.BlockSpec((pair * VH, LAT), lambda h, p: (h, 0)),
            ],
            out_specs=pl.BlockSpec((group_rows, pair * VH), lambda h, p: (0, h)),
            scratch_shapes=[
                pltpu.VMEM((pair, 1, group_rows), jnp.float32),
                pltpu.VMEM((pair, 1, group_rows), jnp.float32),
                pltpu.VMEM((pair, VH, group_rows), jnp.float32),
            ],
        ),
        compiler_params=pltpu.CompilerParams(vmem_limit_bytes=40 * 1024 * 1024),
        cost_estimate=pl.CostEstimate(
            flops=2 * heads * group_rows * row_count * 4 * NOPE,
            bytes_accessed=row_count * (LAT + ROPE) * 4,
            transcendentals=heads * group_rows * row_count,
        ),
        name="prefill_attend",
    )(seq_index.reshape(1).astype(jnp.int32), queries, rows, key_expand, value_expand.T)


def gather_body(owners, own_ref, all_ref, send_sem, recv_sem, local_sem):
    me = lax.axis_index("seq")
    rows = own_ref.shape[0]
    barrier = pltpu.get_barrier_semaphore()
    for step in range(1, owners):
        peer = lax.rem(me + step, owners)
        pl.semaphore_signal(
            barrier, inc=1, device_id={"seq": peer}, device_id_type=pl.DeviceIdType.MESH
        )
    pl.semaphore_wait(barrier, owners - 1)
    place = all_ref.at[pl.ds(pl.multiple_of(me * rows, rows), rows)]
    copies = []
    for step in range(1, owners):
        peer = lax.rem(me + step, owners)
        copies.append(
            pltpu.make_async_remote_copy(
                src_ref=own_ref,
                dst_ref=place,
                send_sem=send_sem.at[step],
                recv_sem=recv_sem.at[step],
                device_id={"seq": peer},
                device_id_type=pl.DeviceIdType.MESH,
            )
        )
        copies[-1].start()
    local = pltpu.make_async_copy(own_ref, place, local_sem)
    local.start()
    local.wait()
    for copy in copies:
        copy.wait()


def gather_rows(own, owners):
    rows, width = own.shape
    return pl.pallas_call(
        functools.partial(gather_body, owners),
        out_shape=jax.ShapeDtypeStruct((owners * rows, width), own.dtype),
        in_specs=[pl.BlockSpec(memory_space=pltpu.VMEM)],
        out_specs=pl.BlockSpec(memory_space=pltpu.VMEM),
        scratch_shapes=[
            pltpu.SemaphoreType.DMA((owners,)),
            pltpu.SemaphoreType.DMA((owners,)),
            pltpu.SemaphoreType.DMA,
        ],
        compiler_params=pltpu.CompilerParams(collective_id=0, has_side_effects=True),
        name="gather_rows",
    )(own)


def query_body(rows_ref, weight_ref, key_ref, cos_ref, sin_ref, prefill_ref, decode_ref):
    pair, group_rows, _ = prefill_ref.shape
    owners, slab, _ = decode_ref.shape
    each = slab // pair
    nt = (((1,), (1,)), ((), ()))
    projected = jnp.dot(rows_ref[...], weight_ref[...], preferred_element_type=jnp.float32)
    for h in range(pair):
        start = h * (NOPE + ROPE)
        nope = projected[:, start : start + NOPE].astype(jnp.bfloat16)
        rope = projected[:, start + NOPE : start + NOPE + ROPE]
        turned = jnp.concatenate([rope[:, ROPE // 2 :], rope[:, : ROPE // 2]], axis=1)
        rope = (rope * cos_ref[...] + turned * sin_ref[...]).astype(jnp.bfloat16)
        prefill_ref[h] = jnp.concatenate([nope[:group_rows], rope[:group_rows]], axis=1)
        latent = lax.dot_general(
            nope[group_rows:],
            key_ref[:, h * NOPE : (h + 1) * NOPE],
            nt,
            preferred_element_type=jnp.float32,
        ).astype(jnp.bfloat16)
        full = jnp.concatenate([latent, rope[group_rows:]], axis=1)
        decode_ref[:, h * each : (h + 1) * each, :] = full.reshape(owners, each, LAT + ROPE)


def make_queries(rows, group_rows, owners, query_proj, key_expand, cosine, sine):
    pair = 2
    total, width = rows.shape
    heads = key_expand.shape[1] // NOPE
    each = (total - group_rows) // owners
    return pl.pallas_call(
        query_body,
        out_shape=(
            jax.ShapeDtypeStruct((heads, group_rows, NOPE + ROPE), jnp.bfloat16),
            jax.ShapeDtypeStruct((owners, heads * each, LAT + ROPE), jnp.bfloat16),
        ),
        grid=(heads // pair,),
        in_specs=[
            pl.BlockSpec((total, width), lambda h: (0, 0)),
            pl.BlockSpec((width, pair * (NOPE + ROPE)), lambda h: (0, h)),
            pl.BlockSpec((LAT, pair * NOPE), lambda h: (0, h)),
            pl.BlockSpec((total, ROPE), lambda h: (0, 0)),
            pl.BlockSpec((total, ROPE), lambda h: (0, 0)),
        ],
        out_specs=(
            pl.BlockSpec((pair, group_rows, NOPE + ROPE), lambda h: (h, 0, 0)),
            pl.BlockSpec((owners, pair * each, LAT + ROPE), lambda h: (0, h, 0)),
        ),
        compiler_params=pltpu.CompilerParams(vmem_limit_bytes=40 * 1024 * 1024),
        cost_estimate=pl.CostEstimate(
            flops=2 * total * width * query_proj.shape[1],
            bytes_accessed=2 * width * (query_proj.shape[1] + total),
            transcendentals=0,
        ),
        name="make_queries",
    )(rows, query_proj, key_expand, cosine, sine)


def page_body(reqs, query_ref, page_ref, holder_ref, value_ref, out_ref, parts, logs):
    owner = pl.program_id(0)
    heads, _, _ = parts.shape
    rows = query_ref.shape[1]
    each = rows // heads
    keys = page_ref[0]
    nt = (((1,), (1,)), ((), ()))
    scores = lax.dot_general(query_ref[0], keys, nt, preferred_element_type=jnp.float32)
    request = lax.rem(lax.broadcasted_iota(jnp.int32, (rows, 1), 0), reqs)
    live = holder_ref[0] == request
    scores = jnp.where(live, scores * (NOPE + ROPE) ** (-0.5), masked_score)
    highest = jnp.max(scores, axis=1, keepdims=True)
    weights = jnp.where(live, jnp.exp(scores - highest), 0.0)
    totals = jnp.sum(weights, axis=1, keepdims=True)
    safe = jnp.maximum(totals, 1e-30)
    summed = jnp.dot(weights.astype(jnp.bfloat16), keys[:, :LAT], preferred_element_type=jnp.float32)
    summed = (summed / safe).astype(jnp.bfloat16)
    place = pl.ds(pl.multiple_of(owner * each, each), each)
    parts[:, place, :] = summed.reshape(heads, each, LAT)
    log = jnp.where(totals > 0, highest + jnp.log(safe), masked_score)
    logs[:, place, :] = log.reshape(heads, each, 1)

    @pl.when(owner == pl.num_programs(0) - 1)
    def _():
        lane = lax.broadcasted_iota(jnp.int32, (parts.shape[1], 128), 1)
        tail = jnp.zeros((parts.shape[1], 128), jnp.float32)
        for h in range(heads):
            out_ref[:, h * VH : (h + 1) * VH] = jnp.dot(
                parts[h], value_ref[:, h * VH : (h + 1) * VH], preferred_element_type=jnp.float32
            ).astype(out_ref.dtype)
            high = logs[h].astype(jnp.bfloat16).astype(jnp.float32)
            tail = jnp.where(lane == h, high, tail)
            tail = jnp.where(lane == heads + h, logs[h] - high, tail)
        out_ref[:, heads * VH :] = tail.astype(out_ref.dtype)


def attend_pages(reqs, queries, pages, holders, value_expand):
    owners, rows, depth = queries.shape
    heads = value_expand.shape[1] // VH
    keys = pages.shape[1]
    total = owners * rows // heads
    return pl.pallas_call(
        functools.partial(page_body, reqs),
        out_shape=jax.ShapeDtypeStruct((total, heads * VH + 128), jnp.bfloat16),
        grid=(owners,),
        in_specs=[
            pl.BlockSpec((1, rows, depth), lambda o: (o, 0, 0)),
            pl.BlockSpec((1, keys, depth), lambda o: (o, 0, 0)),
            pl.BlockSpec((1, 1, keys), lambda o: (o, 0, 0)),
            pl.BlockSpec(value_expand.shape, lambda o: (0, 0)),
        ],
        out_specs=pl.BlockSpec((total, heads * VH + 128), lambda o: (0, 0)),
        scratch_shapes=[
            pltpu.VMEM((heads, total, LAT), jnp.bfloat16),
            pltpu.VMEM((heads, total, 1), jnp.float32),
        ],
        compiler_params=pltpu.CompilerParams(vmem_limit_bytes=40 * 1024 * 1024),
        cost_estimate=pl.CostEstimate(
            flops=4 * owners * rows * keys * depth,
            bytes_accessed=2 * owners * keys * depth,
            transcendentals=owners * rows * keys,
        ),
        name="attend_pages",
    )(queries, pages, holders, value_expand)


def merge_body(reqs, count, came_ref, query_ref, fresh_ref, value_ref, weight_ref, out_ref):
    owners, each, _ = came_ref.shape
    heads = query_ref.shape[0]
    pieces, _, share = out_ref.shape
    nt = (((1,), (1,)), ((), ()))
    fresh = fresh_ref[...]
    values = jnp.dot(fresh[:, :LAT], value_ref[...], preferred_element_type=jnp.float32)
    values = values.astype(jnp.bfloat16)
    row = lax.broadcasted_iota(jnp.int32, (each, each), 0)
    col = lax.broadcasted_iota(jnp.int32, (each, each), 1)
    live = (lax.rem(row, reqs) == lax.rem(col, reqs)) & (col <= row) & (col < count)
    logs = [came_ref[s, :, heads * VH :].astype(jnp.float32) for s in range(owners)]
    results = []
    for h in range(heads):
        scores = lax.dot_general(query_ref[h], fresh, nt, preferred_element_type=jnp.float32)
        scores = jnp.where(live, scores * (NOPE + ROPE) ** (-0.5), masked_score)
        log = [g[:, h : h + 1] + g[:, heads + h : heads + h + 1] for g in logs]
        top = jnp.max(scores, axis=1, keepdims=True)
        for one in log:
            top = jnp.maximum(top, one)
        weights = jnp.where(live, jnp.exp(scores - top), 0.0)
        total = jnp.sum(weights, axis=1, keepdims=True)
        cut = slice(h * VH, (h + 1) * VH)
        mixed = jnp.dot(
            weights.astype(jnp.bfloat16), values[:, cut], preferred_element_type=jnp.float32
        )
        for s in range(owners):
            factor = jnp.exp(log[s] - top)
            total = total + factor
            mixed = mixed + factor * came_ref[s, :, cut].astype(jnp.float32)
        results.append((mixed / total).astype(jnp.bfloat16))
    part = jnp.dot(
        jnp.concatenate(results, axis=1), weight_ref[...], preferred_element_type=jnp.float32
    )
    for p in range(pieces):
        out_ref[p] = part[:, p * share : (p + 1) * share].astype(out_ref.dtype)


def merge_parts(reqs, count, pieces, came, queries, fresh, value_expand, mla_output):
    each = came.shape[1]
    share = mla_output.shape[1] // pieces
    return pl.pallas_call(
        functools.partial(merge_body, reqs, count),
        out_shape=jax.ShapeDtypeStruct((pieces, each, share), jnp.bfloat16),
        in_specs=[pl.BlockSpec(memory_space=pltpu.VMEM)] * 5,
        out_specs=pl.BlockSpec(memory_space=pltpu.VMEM),
        compiler_params=pltpu.CompilerParams(vmem_limit_bytes=40 * 1024 * 1024),
        name="merge_parts",
    )(came, queries, fresh, value_expand, mla_output)


def sum_body(members, gather, part_ref, *refs):
    if gather:
        out_ref, came, send_sem, recv_sem, send_back, recv_back = refs
    else:
        base_ref, out_ref, came, send_sem, recv_sem = refs
    me = lax.axis_index("grp")
    peers = [lax.rem(me + step, members) for step in range(members)]
    barrier = pltpu.get_barrier_semaphore()
    for peer in peers[1:]:
        pl.semaphore_signal(
            barrier, inc=1, device_id={"grp": peer}, device_id_type=pl.DeviceIdType.MESH
        )
    pl.semaphore_wait(barrier, members - 1)
    copies = []
    for step in range(1, members):
        copies.append(
            pltpu.make_async_remote_copy(
                src_ref=part_ref.at[peers[step]],
                dst_ref=came.at[step],
                send_sem=send_sem.at[step],
                recv_sem=recv_sem.at[step],
                device_id={"grp": peers[step]},
                device_id_type=pl.DeviceIdType.MESH,
            )
        )
        copies[-1].start()
    total = part_ref[me].astype(jnp.float32)
    for step in range(1, members):
        copies[step - 1].wait()
        total = total + came[step].astype(jnp.float32)
    if not gather:
        out_ref[...] = (base_ref[...] + total).astype(out_ref.dtype)
        return
    out_ref[me] = total.astype(out_ref.dtype)
    copies = []
    for step in range(1, members):
        copies.append(
            pltpu.make_async_remote_copy(
                src_ref=out_ref.at[me],
                dst_ref=out_ref.at[me],
                send_sem=send_back.at[step],
                recv_sem=recv_back.at[step],
                device_id={"grp": peers[step]},
                device_id_type=pl.DeviceIdType.MESH,
            )
        )
        copies[-1].start()
    for copy in copies:
        copy.wait()


def sum_over_grp(parts, base=None):
    members, rows, share = parts.shape
    gather = base is None
    sems = [pltpu.SemaphoreType.DMA((members,))] * (4 if gather else 2)
    operands = (parts,) if gather else (parts, base)
    return pl.pallas_call(
        functools.partial(sum_body, members, gather),
        out_shape=jax.ShapeDtypeStruct(parts.shape if gather else (rows, share), jnp.bfloat16),
        in_specs=[pl.BlockSpec(memory_space=pltpu.VMEM)] * len(operands),
        out_specs=pl.BlockSpec(memory_space=pltpu.VMEM),
        scratch_shapes=[pltpu.VMEM(parts.shape, jnp.bfloat16)] + sems,
        compiler_params=pltpu.CompilerParams(
            collective_id=1 if gather else 2, has_side_effects=True
        ),
        name="sum_hidden" if gather else "sum_output",
    )(*operands)


def delta_body(
    steps,
    reqs,
    hidden_ref,
    input_ref,
    beta_ref,
    decay_down_ref,
    decay_up_ref,
    gate_down_ref,
    gate_up_ref,
    rate_ref,
    state_ref,
    output_ref,
    out_ref,
    kin,
    decay_low,
    gate_low,
    betas,
    total,
):
    turn = pl.program_id(0)
    sources, _, pair, _, _ = state_ref.shape
    each = hidden_ref.shape[0]
    pieces, _, share = out_ref.shape
    f32, bf16 = jnp.float32, jnp.bfloat16
    nt = (((1,), (1,)), ((), ()))

    @pl.when(turn == 0)
    def _():
        kin[...] = norm_rows(hidden_ref[...]).astype(bf16)
        rows = kin[...]
        decay_low[...] = jnp.dot(rows, decay_down_ref[...], preferred_element_type=f32).astype(bf16)
        gate_low[...] = jnp.dot(rows, gate_down_ref[...], preferred_element_type=f32).astype(bf16)
        betas[...] = jax.nn.sigmoid(jnp.dot(rows, beta_ref[...], preferred_element_type=f32))
        total[...] = jnp.zeros_like(total)

    rows = kin[...]
    query, key, value = [jnp.dot(rows, input_ref[i], preferred_element_type=f32) for i in range(3)]
    raw = jnp.dot(decay_low[...], decay_up_ref[...], preferred_element_type=f32)
    soft = jnp.maximum(raw, 0.0) + jnp.log1p(jnp.exp(-jnp.abs(raw)))
    decays = jnp.exp(-rate_ref[...] * soft)
    gate = jax.nn.sigmoid(jnp.dot(gate_low[...], gate_up_ref[...], preferred_element_type=f32))
    lane = lax.broadcasted_iota(jnp.int32, betas.shape, 1)
    owner_row = lax.rem(lax.broadcasted_iota(jnp.int32, (2 * steps * reqs, 1), 0), reqs)
    results = []
    for h in range(pair):
        cut = slice(h * DK, (h + 1) * DK)
        beta = jnp.sum(
            jnp.where(lane == turn * pair + h, betas[...], 0.0), axis=1, keepdims=True
        )
        units = (unit_rows(key[:, cut]), unit_rows(query[:, cut]) * DK ** (-0.5))
        at = [slice(t * reqs, (t + 1) * reqs) for t in range(steps)]
        keys = [units[0][a] for a in at]
        queries = [units[1][a] for a in at]
        decay = [decays[a, cut] for a in at]
        grown = [decay[0]]
        for t in range(1, steps):
            grown.append(grown[-1] * decay[t])
        looks = jnp.concatenate(
            [keys[t] * grown[t] for t in range(steps)]
            + [queries[t] * grown[t] for t in range(steps)],
            axis=0,
        ).astype(bf16)
        seen = jnp.zeros(looks.shape, f32)
        for r in range(reqs):
            state = state_ref[:, r, h].reshape(DV, DK)
            found = lax.dot_general(looks, state, nt, preferred_element_type=f32)
            seen = jnp.where(owner_row == r, found, seen)
        written = []
        reads = []
        for t in range(steps):
            if t:
                written = [(e, k * decay[t]) for e, k in written]
            err = value[at[t], cut] - seen[t * reqs : (t + 1) * reqs]
            for e, k in written:
                err = err - e * jnp.sum(k * keys[t], axis=1, keepdims=True)
            written.append((beta[at[t]] * err, keys[t]))
            read = seen[(steps + t) * reqs : (steps + t + 1) * reqs]
            for e, k in written:
                read = read + e * jnp.sum(k * queries[t], axis=1, keepdims=True)
            reads.append(norm_rows(read) * gate[at[t], cut])
        reads.append(jnp.zeros((each - steps * reqs, DV), f32))
        results.append(jnp.concatenate(reads, axis=0).astype(bf16))
    total[...] += jnp.dot(
        jnp.concatenate(results, axis=1), output_ref[...], preferred_element_type=f32
    )

    @pl.when(turn == pl.num_programs(0) - 1)
    def _():
        for p in range(pieces):
            out_ref[p] = total[:, p * share : (p + 1) * share].astype(out_ref.dtype)


def delta_steps(
    steps,
    reqs,
    pieces,
    hidden,
    kda_inputs,
    kda_beta,
    decay_down,
    decay_up,
    gate_down,
    gate_up,
    rate,
    states,
    kda_output,
):
    each, width = hidden.shape
    heads = kda_beta.shape[1]
    pair = 2
    sources, _, _, part, _ = states.shape
    whole = lambda h: (0, 0)
    wide = lambda h: (0, h)
    return pl.pallas_call(
        functools.partial(delta_body, steps, reqs),
        out_shape=jax.ShapeDtypeStruct((pieces, each, width // pieces), jnp.bfloat16),
        grid=(heads // pair,),
        in_specs=[
            pl.BlockSpec((each, width), whole),
            pl.BlockSpec((3, width, pair * DK), lambda h: (0, 0, h)),
            pl.BlockSpec((width, heads), whole),
            pl.BlockSpec(decay_down.shape, whole),
            pl.BlockSpec((decay_up.shape[0], pair * DK), wide),
            pl.BlockSpec(gate_down.shape, whole),
            pl.BlockSpec((gate_up.shape[0], pair * DV), wide),
            pl.BlockSpec((1, pair * DK), wide),
            pl.BlockSpec((sources, reqs, pair, part, DK), lambda h: (0, 0, h, 0, 0)),
            pl.BlockSpec((pair * DV, width), lambda h: (h, 0)),
        ],
        out_specs=pl.BlockSpec((pieces, each, width // pieces), lambda h: (0, 0, 0)),
        scratch_shapes=[
            pltpu.VMEM((each, width), jnp.bfloat16),
            pltpu.VMEM((each, decay_down.shape[1]), jnp.bfloat16),
            pltpu.VMEM((each, gate_down.shape[1]), jnp.bfloat16),
            pltpu.VMEM((each, heads), jnp.float32),
            pltpu.VMEM((each, width), jnp.float32),
        ],
        compiler_params=pltpu.CompilerParams(vmem_limit_bytes=40 * 1024 * 1024),
        name="delta_steps",
    )(
        hidden,
        kda_inputs,
        kda_beta,
        decay_down,
        decay_up,
        gate_down,
        gate_up,
        rate,
        states,
        kda_output,
    )


def shards(
    x_group,
    decode_input,
    prompt_len,
    latent_pages,
    slot_target,
    page_counts,
    kda_state,
    query_proj,
    latent_proj,
    key_expand,
    value_expand,
    mla_output,
    kda_inputs,
    kda_beta,
    decay_down,
    decay_up,
    gate_down,
    gate_up,
    decay_log,
    kda_output,
):
    f32, bf16 = jnp.float32, jnp.bfloat16
    seq_index = lax.axis_index("seq")
    grp_index = lax.axis_index("grp")
    owners = lax.axis_size("seq")
    heads = key_expand.shape[1] // NOPE
    width = x_group.shape[1]
    share = width // lax.axis_size("grp")
    col = grp_index * share
    steps, reqs, _ = decode_input.shape
    cap = slot_target.shape[2]
    n = steps * reqs

    dec_own = decode_input.reshape(n, width)
    group_rows = x_group.shape[0]
    rows_share = group_rows // lax.axis_size("grp")
    x_normed = norm_rows(x_group.astype(f32)).astype(bf16)
    own_normed = norm_rows(dec_own.astype(f32)).astype(bf16)
    own_place = (prompt_len[None, :] + jnp.arange(steps)[:, None]).reshape(n)
    share_normed = lax.dynamic_slice_in_dim(x_normed, grp_index * rows_share, rows_share, 0)
    share_place = seq_index * group_rows + grp_index * rows_share + jnp.arange(rows_share)
    latents = make_latent(
        jnp.concatenate([share_normed, own_normed]),
        latent_proj,
        jnp.concatenate([share_place, own_place]),
    )
    fresh = latents[rows_share:]
    shard_rows = lax.all_gather(latents[:rows_share], ("seq", "grp"), axis=0, tiled=True)

    each = -(-(n + 1) // 16) * 16
    numbers = jnp.concatenate(
        [prompt_len // PAGE, prompt_len % PAGE, page_counts[:, 0], slot_target.reshape(-1)]
    ).astype(bf16)
    numbers = jnp.pad(numbers, (0, width - numbers.shape[0]))[None]
    payload = jnp.concatenate(
        [own_normed, numbers, jnp.zeros((each - n - 1, width), bf16)], axis=0
    )
    payload, latents = lax.optimization_barrier((payload, latents))
    dec_all = gather_rows(payload, owners)
    numbers = dec_all.reshape(owners, each, width)[:, n, : 2 * reqs + owners + owners * cap]
    ints = numbers.astype(jnp.int32)
    lens_all = ints[:, :reqs] * PAGE + ints[:, reqs : 2 * reqs]
    counts = lax.dynamic_slice_in_dim(ints, 2 * reqs + seq_index, 1, 1)
    targets = lax.dynamic_slice_in_dim(ints, 2 * reqs + owners + seq_index * cap, cap, 1)

    states = kda_state.astype(bf16).reshape((owners, reqs) + kda_state.shape[1:])
    states = lax.all_to_all(states, "seq", split_axis=0, concat_axis=0, tiled=True)

    position = seq_index * group_rows + jnp.arange(group_rows)
    dec_place = (lens_all[:, None, :] + jnp.arange(each // reqs)[None, :, None]).reshape(-1)
    place = jnp.concatenate([position, dec_place]).astype(f32)
    half = ROPE // 2
    angles = place[:, None] * jnp.exp(-jnp.log(10000.0) * jnp.arange(half, dtype=f32) / half)
    cosine, sine = jnp.cos(angles), jnp.sin(angles)
    queries, qc = make_queries(
        jnp.concatenate([x_normed, dec_all]),
        group_rows,
        owners,
        query_proj,
        key_expand,
        jnp.concatenate([cosine, cosine], axis=1),
        jnp.concatenate([-sine, sine], axis=1),
    )

    pages = latent_pages.reshape(owners, cap * PAGE, LAT + ROPE)
    token = (targets % MAXP)[..., None] * PAGE + jnp.arange(PAGE)
    holder = targets // MAXP
    length = jnp.sum(
        jnp.where(holder[..., None] == jnp.arange(reqs), lens_all[:, None, :], 0), axis=-1
    )
    live = (jnp.arange(cap)[None, :] < counts)[..., None] & (token < length[..., None])
    holders = jnp.where(live, holder[..., None], -1).reshape(owners, 1, cap * PAGE)
    sent = attend_pages(reqs, qc, pages, holders, value_expand)
    sent, shard_rows = lax.optimization_barrier((sent, shard_rows))
    came = lax.all_to_all(
        sent.reshape(owners, each, -1), "seq", split_axis=0, concat_axis=0, tiled=True
    )

    heads_out = prefill_attend(seq_index, queries, shard_rows, key_expand, value_expand)
    prefill_part = jnp.dot(heads_out, mla_output, preferred_element_type=f32)
    came, prefill_part = lax.optimization_barrier((came, prefill_part))
    attended = lax.psum_scatter(
        prefill_part.astype(bf16), "grp", scatter_dimension=1, tiled=True
    )

    pieces = lax.axis_size("grp")
    fresh = jnp.pad(fresh, ((0, each - n), (0, 0)))
    own_query = lax.dynamic_index_in_dim(qc, seq_index, 0, keepdims=False)
    own_query = own_query.reshape(heads, each, LAT + ROPE)
    mla_parts = merge_parts(
        reqs, n, pieces, came, own_query, fresh, value_expand, mla_output
    )
    mla_total = sum_over_grp(mla_parts)
    dec_rows = jnp.pad(dec_own, ((0, each - n), (0, 0))).astype(f32)
    hidden = dec_rows + mla_total.transpose(1, 0, 2).reshape(each, width).astype(f32)

    kda_parts = delta_steps(
        steps,
        reqs,
        pieces,
        hidden,
        kda_inputs.transpose(1, 0, 2),
        kda_beta,
        decay_down,
        decay_up,
        gate_down,
        gate_up,
        jnp.repeat(jnp.exp(decay_log), DK)[None],
        states,
        kda_output,
    )
    kda_parts, attended = lax.optimization_barrier((kda_parts, attended))
    decode_out = sum_over_grp(kda_parts, lax.dynamic_slice_in_dim(hidden, col, share, 1))
    prefill_out = (
        lax.dynamic_slice_in_dim(x_group, col, share, 1).astype(f32) + attended.astype(f32)
    ).astype(bf16)
    return (prefill_out, decode_out[:n].reshape(steps, reqs, share))


def solution(mesh):
    in_specs = (
        P("seq", None),
        P(None, "seq", None),
        P("seq"),
        P("seq", None, None, None, None),
        P(None, "seq", None),
        P(None, "seq"),
        P(None, "grp", "seq", None),
        P(None, "grp"),
        P(),
        P(None, "grp"),
        P(None, "grp"),
        P("grp", None),
        P(None, None, "grp"),
        P(None, "grp"),
        P(),
        P(None, "grp"),
        P(),
        P(None, "grp"),
        P("grp"),
        P("grp", None),
    )
    out_specs = (P("seq", "grp"), P(None, "seq", "grp"))
    return jax.shard_map(shards, mesh=mesh, in_specs=in_specs, out_specs=out_specs, check_vma=False)
```

```python
import functools

import jax
import jax.numpy as jnp
from jax import lax
from jax.experimental import pallas as pl
from jax.experimental.pallas import tpu as pltpu
from jax.sharding import PartitionSpec as P

LAT = 512
ROPE = 64
NOPE = 128
VH = 128
DK = 128
DV = 128
PAGE = 64
MAXP = 12


epsilon = 1e-06
masked_score = -1e30


def norm_rows(values):
    return values * lax.rsqrt(jnp.mean(values * values, axis=-1, keepdims=True) + epsilon)


def unit_rows(values):
    return values * lax.rsqrt(jnp.sum(values * values, axis=-1, keepdims=True) + epsilon)


def rotate(values, position):
    halfway = values.shape[-1] // 2
    frequency = jnp.exp(-jnp.log(10000.0) * jnp.arange(halfway, dtype=jnp.float32) / halfway)
    angles = position.astype(jnp.float32)[..., None] * frequency
    leading = values[..., :halfway]
    trailing = values[..., halfway:]
    return jnp.concatenate(
        [
            leading * jnp.cos(angles) - trailing * jnp.sin(angles),
            leading * jnp.sin(angles) + trailing * jnp.cos(angles),
        ],
        axis=-1,
    )


def make_latent(normed, latent_proj, position):
    projected = jnp.dot(normed, latent_proj, preferred_element_type=jnp.float32)
    return jnp.concatenate(
        [norm_rows(projected[:, :LAT]), rotate(projected[:, LAT:], position)], axis=-1
    ).astype(jnp.bfloat16)


def make_query(normed, query_proj, position):
    head_count = query_proj.shape[1] // (NOPE + ROPE)
    projected = jnp.dot(normed, query_proj, preferred_element_type=jnp.float32).reshape(
        normed.shape[0], head_count, NOPE + ROPE
    )
    return (
        projected[..., :NOPE].astype(jnp.bfloat16),
        rotate(projected[..., NOPE:], position[:, None]).astype(jnp.bfloat16),
    )


def prefill_body(place_ref, query_ref, rows_ref, key_ref, value_ref, out_ref, peak, total, mixed):
    pair, group_rows, _ = query_ref.shape
    nt = (((1,), (1,)), ((), ()))
    factor = (NOPE + ROPE) ** (-0.5) * 1.4426950408889634
    own = place_ref[0]

    def chunk(index, first):
        rows = rows_ref[pl.ds(pl.multiple_of(index * group_rows, group_rows), group_rows), :]
        latent = rows[:, :LAT]
        keys = jnp.dot(latent, key_ref[...], preferred_element_type=jnp.float32)
        keys = keys.astype(jnp.bfloat16)
        values = lax.dot_general(value_ref[...], latent, nt, preferred_element_type=jnp.float32)
        values = values.astype(jnp.bfloat16)
        for h in range(pair):
            full = jnp.concatenate([keys[:, h * NOPE : (h + 1) * NOPE], rows[:, LAT:]], axis=1)
            scores = lax.dot_general(full, query_ref[h], nt, preferred_element_type=jnp.float32)
            if first:
                key_at = lax.broadcasted_iota(jnp.int32, scores.shape, 0)
                query_at = lax.broadcasted_iota(jnp.int32, scores.shape, 1)
                scores = jnp.where(key_at <= query_at, scores, masked_score)
            top = jnp.max(scores, axis=0, keepdims=True)
            if not first:
                top = jnp.maximum(top, peak[h])
            weights = jnp.exp2((scores - top) * factor)
            summed = jnp.sum(weights, axis=0, keepdims=True)
            added = jnp.dot(
                values[h * VH : (h + 1) * VH],
                weights.astype(jnp.bfloat16),
                preferred_element_type=jnp.float32,
            )
            if first:
                total[h] = summed
                mixed[h] = added
            else:
                shrink = jnp.exp2((peak[h] - top) * factor)
                total[h] = total[h] * shrink + summed
                mixed[h] = mixed[h] * shrink + added
            peak[h] = top

    chunk(own, True)

    @pl.loop(0, own)
    def _(index):
        chunk(index, False)

    for h in range(pair):
        out_ref[:, h * VH : (h + 1) * VH] = (mixed[h] / total[h]).T.astype(out_ref.dtype)


def prefill_attend(seq_index, queries, rows, key_expand, value_expand):
    heads, group_rows, _ = queries.shape
    pair = 4 if heads % 4 == 0 else 2
    row_count = rows.shape[0]
    return pl.pallas_call(
        prefill_body,
        out_shape=jax.ShapeDtypeStruct((group_rows, heads * VH), jnp.bfloat16),
        grid_spec=pltpu.PrefetchScalarGridSpec(
            num_scalar_prefetch=1,
            grid=(heads // pair,),
            in_specs=[
                pl.BlockSpec((pair, group_rows, NOPE + ROPE), lambda h, p: (h, 0, 0)),
                pl.BlockSpec((row_count, LAT + ROPE), lambda h, p: (0, 0)),
                pl.BlockSpec((LAT, pair * NOPE), lambda h, p: (0, h)),
                pl.BlockSpec((pair * VH, LAT), lambda h, p: (h, 0)),
            ],
            out_specs=pl.BlockSpec((group_rows, pair * VH), lambda h, p: (0, h)),
            scratch_shapes=[
                pltpu.VMEM((pair, 1, group_rows), jnp.float32),
                pltpu.VMEM((pair, 1, group_rows), jnp.float32),
                pltpu.VMEM((pair, VH, group_rows), jnp.float32),
            ],
        ),
        compiler_params=pltpu.CompilerParams(vmem_limit_bytes=40 * 1024 * 1024),
        cost_estimate=pl.CostEstimate(
            flops=2 * heads * group_rows * row_count * 4 * NOPE,
            bytes_accessed=row_count * (LAT + ROPE) * 4,
            transcendentals=heads * group_rows * row_count,
        ),
        name="prefill_attend",
    )(seq_index.reshape(1).astype(jnp.int32), queries, rows, key_expand, value_expand.T)


def gather_body(sizes, own_ref, all_ref, *sems):
    zs, ys, xs, cs = sizes
    z_send, z_recv, y_send, y_recv, x_send, x_recv, c_send, c_recv, local_sem = sems
    seq_at, grp_at = lax.axis_index("seq"), lax.axis_index("grp")
    z, y = seq_at // ys, lax.rem(seq_at, ys)
    x, c = grp_at // cs, lax.rem(grp_at, cs)

    def seq_of(dz, dy):
        return lax.rem(z + dz + zs, zs) * ys + lax.rem(y + dy + ys, ys)

    def grp_of(dx, dc):
        return lax.rem(x + dx + xs, xs) * cs + lax.rem(c + dc + cs, cs)

    z_peers = [{"seq": seq_of(d, 0)} for d in range(zs)]
    y_peers = [{"seq": seq_of(0, d)} for d in range(ys)]
    x_peers = [{"grp": grp_of(d, 0)} for d in range(xs)]
    c_peers = [{"grp": grp_of(0, d)} for d in range(cs)]
    peers = z_peers[1:] + y_peers[1:] + x_peers[1:] + c_peers[1:]
    barrier = pltpu.get_barrier_semaphore()
    for peer in peers:
        pl.semaphore_signal(
            barrier, inc=1, device_id=peer, device_id_type=pl.DeviceIdType.MESH
        )
    pl.semaphore_wait(barrier, len(peers))

    started = []

    def push(back, peer, send, recv):
        dz, dy, dx = back
        place = all_ref.at[seq_of(-dz, -dy), grp_of(-dx, 0)]
        copy = pltpu.make_async_remote_copy(
            src_ref=place if any(back) else own_ref,
            dst_ref=place,
            send_sem=send,
            recv_sem=recv,
            device_id=peer,
            device_id_type=pl.DeviceIdType.MESH,
        )
        copy.start()
        started.append(copy)
        return copy

    by_z, by_y, by_x, by_c = {}, {}, {}, {}

    def across(dz, dy):
        for d in range(1, xs):
            at = (d, dz, dy)
            by_x[at] = push((dz, dy, 0), x_peers[d], x_send.at[at], x_recv.at[at])
        to_core(0, dz, dy)

    def to_core(dx, dz, dy):
        for d in range(1, cs):
            at = (dx, dz, dy)
            by_c[(d,) + at] = push((dz, dy, dx), c_peers[d], c_send.at[at], c_recv.at[at])

    def along(dz):
        for d in range(1, ys):
            by_y[d, dz] = push((dz, 0, 0), y_peers[d], y_send.at[d, dz], y_recv.at[d, dz])
        across(dz, 0)

    local = pltpu.make_async_copy(own_ref, all_ref.at[seq_at, grp_at], local_sem)
    local.start()
    for d in range(1, zs):
        by_z[d] = push((0, 0, 0), z_peers[d], z_send.at[d], z_recv.at[d])
    along(0)
    for dz in range(1, zs):
        by_z[dz].wait_recv()
        along(dz)
    for dz in range(zs):
        for dy in range(1, ys):
            by_y[dy, dz].wait_recv()
            across(dz, dy)
    for at in list(by_x):
        by_x[at].wait_recv()
        to_core(*at)
    for copy in by_c.values():
        copy.wait_recv()
    local.wait()
    for copy in started:
        copy.wait_send()


def gather_blocks(own, owners, members):
    rows, width = own.shape
    cs = 2 if members % 2 == 0 else 1
    zs = 4 if owners % 4 == 0 else owners
    sizes = (zs, owners // zs, members // cs, cs)
    zs, ys, xs, cs = sizes
    shapes = [(zs,), (ys, zs), (xs, zs, ys), (xs, zs, ys)]
    sems = [pltpu.SemaphoreType.DMA(shape) for shape in shapes for _ in range(2)]
    return pl.pallas_call(
        functools.partial(gather_body, sizes),
        out_shape=jax.ShapeDtypeStruct((owners, members, rows, width), own.dtype),
        in_specs=[pl.BlockSpec(memory_space=pltpu.VMEM)],
        out_specs=pl.BlockSpec(memory_space=pltpu.VMEM),
        scratch_shapes=sems + [pltpu.SemaphoreType.DMA],
        compiler_params=pltpu.CompilerParams(
            collective_id=0, has_side_effects=True, vmem_limit_bytes=40 * 1024 * 1024
        ),
        name="gather_blocks",
    )(own)


def query_body(rows_ref, weight_ref, key_ref, cos_ref, sin_ref, prefill_ref, decode_ref):
    pair, group_rows, _ = prefill_ref.shape
    owners, slab, _ = decode_ref.shape
    each = slab // pair
    nt = (((1,), (1,)), ((), ()))
    projected = jnp.dot(rows_ref[...], weight_ref[...], preferred_element_type=jnp.float32)
    for h in range(pair):
        start = h * (NOPE + ROPE)
        nope = projected[:, start : start + NOPE].astype(jnp.bfloat16)
        rope = projected[:, start + NOPE : start + NOPE + ROPE]
        turned = jnp.concatenate([rope[:, ROPE // 2 :], rope[:, : ROPE // 2]], axis=1)
        rope = (rope * cos_ref[...] + turned * sin_ref[...]).astype(jnp.bfloat16)
        prefill_ref[h] = jnp.concatenate([nope[:group_rows], rope[:group_rows]], axis=1)
        latent = lax.dot_general(
            nope[group_rows:],
            key_ref[:, h * NOPE : (h + 1) * NOPE],
            nt,
            preferred_element_type=jnp.float32,
        ).astype(jnp.bfloat16)
        full = jnp.concatenate([latent, rope[group_rows:]], axis=1)
        decode_ref[:, h * each : (h + 1) * each, :] = full.reshape(owners, each, LAT + ROPE)


def make_queries(rows, group_rows, owners, query_proj, key_expand, cosine, sine):
    pair = 2
    total, width = rows.shape
    heads = key_expand.shape[1] // NOPE
    each = (total - group_rows) // owners
    return pl.pallas_call(
        query_body,
        out_shape=(
            jax.ShapeDtypeStruct((heads, group_rows, NOPE + ROPE), jnp.bfloat16),
            jax.ShapeDtypeStruct((owners, heads * each, LAT + ROPE), jnp.bfloat16),
        ),
        grid=(heads // pair,),
        in_specs=[
            pl.BlockSpec((total, width), lambda h: (0, 0)),
            pl.BlockSpec((width, pair * (NOPE + ROPE)), lambda h: (0, h)),
            pl.BlockSpec((LAT, pair * NOPE), lambda h: (0, h)),
            pl.BlockSpec((total, ROPE), lambda h: (0, 0)),
            pl.BlockSpec((total, ROPE), lambda h: (0, 0)),
        ],
        out_specs=(
            pl.BlockSpec((pair, group_rows, NOPE + ROPE), lambda h: (h, 0, 0)),
            pl.BlockSpec((owners, pair * each, LAT + ROPE), lambda h: (0, h, 0)),
        ),
        compiler_params=pltpu.CompilerParams(vmem_limit_bytes=40 * 1024 * 1024),
        cost_estimate=pl.CostEstimate(
            flops=2 * total * width * query_proj.shape[1],
            bytes_accessed=2 * width * (query_proj.shape[1] + total),
            transcendentals=0,
        ),
        name="make_queries",
    )(rows, query_proj, key_expand, cosine, sine)


def page_body(reqs, query_ref, page_ref, holder_ref, value_ref, out_ref, parts, logs):
    owner = pl.program_id(0)
    heads, _, _ = parts.shape
    rows = query_ref.shape[1]
    each = rows // heads
    keys = page_ref[0]
    nt = (((1,), (1,)), ((), ()))
    scores = lax.dot_general(query_ref[0], keys, nt, preferred_element_type=jnp.float32)
    request = lax.rem(lax.broadcasted_iota(jnp.int32, (rows, 1), 0), reqs)
    live = holder_ref[0] == request
    scores = jnp.where(live, scores * (NOPE + ROPE) ** (-0.5), masked_score)
    highest = jnp.max(scores, axis=1, keepdims=True)
    weights = jnp.where(live, jnp.exp(scores - highest), 0.0)
    totals = jnp.sum(weights, axis=1, keepdims=True)
    safe = jnp.maximum(totals, 1e-30)
    summed = jnp.dot(weights.astype(jnp.bfloat16), keys[:, :LAT], preferred_element_type=jnp.float32)
    summed = (summed / safe).astype(jnp.bfloat16)
    place = pl.ds(pl.multiple_of(owner * each, each), each)
    parts[:, place, :] = summed.reshape(heads, each, LAT)
    log = jnp.where(totals > 0, highest + jnp.log(safe), masked_score)
    logs[:, place, :] = log.reshape(heads, each, 1)

    @pl.when(owner == pl.num_programs(0) - 1)
    def _():
        lane = lax.broadcasted_iota(jnp.int32, (parts.shape[1], 128), 1)
        tail = jnp.zeros((parts.shape[1], 128), jnp.float32)
        for h in range(heads):
            out_ref[:, h * VH : (h + 1) * VH] = jnp.dot(
                parts[h], value_ref[:, h * VH : (h + 1) * VH], preferred_element_type=jnp.float32
            ).astype(out_ref.dtype)
            high = logs[h].astype(jnp.bfloat16).astype(jnp.float32)
            tail = jnp.where(lane == h, high, tail)
            tail = jnp.where(lane == heads + h, logs[h] - high, tail)
        out_ref[:, heads * VH :] = tail.astype(out_ref.dtype)


def attend_pages(reqs, queries, pages, holders, value_expand):
    owners, rows, depth = queries.shape
    heads = value_expand.shape[1] // VH
    keys = pages.shape[1]
    total = owners * rows // heads
    return pl.pallas_call(
        functools.partial(page_body, reqs),
        out_shape=jax.ShapeDtypeStruct((total, heads * VH + 128), jnp.bfloat16),
        grid=(owners,),
        in_specs=[
            pl.BlockSpec((1, rows, depth), lambda o: (o, 0, 0)),
            pl.BlockSpec((1, keys, depth), lambda o: (o, 0, 0)),
            pl.BlockSpec((1, 1, keys), lambda o: (o, 0, 0)),
            pl.BlockSpec(value_expand.shape, lambda o: (0, 0)),
        ],
        out_specs=pl.BlockSpec((total, heads * VH + 128), lambda o: (0, 0)),
        scratch_shapes=[
            pltpu.VMEM((heads, total, LAT), jnp.bfloat16),
            pltpu.VMEM((heads, total, 1), jnp.float32),
        ],
        compiler_params=pltpu.CompilerParams(vmem_limit_bytes=40 * 1024 * 1024),
        cost_estimate=pl.CostEstimate(
            flops=4 * owners * rows * keys * depth,
            bytes_accessed=2 * owners * keys * depth,
            transcendentals=owners * rows * keys,
        ),
        name="attend_pages",
    )(queries, pages, holders, value_expand)


def merge_body(reqs, count, came_ref, query_ref, fresh_ref, value_ref, weight_ref, out_ref):
    owners, each, _ = came_ref.shape
    heads = query_ref.shape[0]
    pieces, _, share = out_ref.shape
    nt = (((1,), (1,)), ((), ()))
    fresh = fresh_ref[...]
    values = jnp.dot(fresh[:, :LAT], value_ref[...], preferred_element_type=jnp.float32)
    values = values.astype(jnp.bfloat16)
    row = lax.broadcasted_iota(jnp.int32, (each, each), 0)
    col = lax.broadcasted_iota(jnp.int32, (each, each), 1)
    live = (lax.rem(row, reqs) == lax.rem(col, reqs)) & (col <= row) & (col < count)
    logs = [came_ref[s, :, heads * VH :].astype(jnp.float32) for s in range(owners)]
    results = []
    for h in range(heads):
        scores = lax.dot_general(query_ref[h], fresh, nt, preferred_element_type=jnp.float32)
        scores = jnp.where(live, scores * (NOPE + ROPE) ** (-0.5), masked_score)
        log = [g[:, h : h + 1] + g[:, heads + h : heads + h + 1] for g in logs]
        top = jnp.max(scores, axis=1, keepdims=True)
        for one in log:
            top = jnp.maximum(top, one)
        weights = jnp.where(live, jnp.exp(scores - top), 0.0)
        total = jnp.sum(weights, axis=1, keepdims=True)
        cut = slice(h * VH, (h + 1) * VH)
        mixed = jnp.dot(
            weights.astype(jnp.bfloat16), values[:, cut], preferred_element_type=jnp.float32
        )
        for s in range(owners):
            factor = jnp.exp(log[s] - top)
            total = total + factor
            mixed = mixed + factor * came_ref[s, :, cut].astype(jnp.float32)
        results.append((mixed / total).astype(jnp.bfloat16))
    part = jnp.dot(
        jnp.concatenate(results, axis=1), weight_ref[...], preferred_element_type=jnp.float32
    )
    for p in range(pieces):
        out_ref[p] = part[:, p * share : (p + 1) * share].astype(out_ref.dtype)


def merge_parts(reqs, count, pieces, came, queries, fresh, value_expand, mla_output):
    each = came.shape[1]
    share = mla_output.shape[1] // pieces
    return pl.pallas_call(
        functools.partial(merge_body, reqs, count),
        out_shape=jax.ShapeDtypeStruct((pieces, each, share), jnp.bfloat16),
        in_specs=[pl.BlockSpec(memory_space=pltpu.VMEM)] * 5,
        out_specs=pl.BlockSpec(memory_space=pltpu.VMEM),
        compiler_params=pltpu.CompilerParams(vmem_limit_bytes=40 * 1024 * 1024),
        name="merge_parts",
    )(came, queries, fresh, value_expand, mla_output)


def sum_body(members, gather, part_ref, *refs):
    if gather:
        out_ref, came, send_sem, recv_sem, send_back, recv_back = refs
    else:
        base_ref, out_ref, came, send_sem, recv_sem = refs
    me = lax.axis_index("grp")
    peers = [lax.rem(me + step, members) for step in range(members)]
    barrier = pltpu.get_barrier_semaphore()
    for peer in peers[1:]:
        pl.semaphore_signal(
            barrier, inc=1, device_id={"grp": peer}, device_id_type=pl.DeviceIdType.MESH
        )
    pl.semaphore_wait(barrier, members - 1)
    copies = []
    for step in range(1, members):
        copies.append(
            pltpu.make_async_remote_copy(
                src_ref=part_ref.at[peers[step]],
                dst_ref=came.at[step],
                send_sem=send_sem.at[step],
                recv_sem=recv_sem.at[step],
                device_id={"grp": peers[step]},
                device_id_type=pl.DeviceIdType.MESH,
            )
        )
        copies[-1].start()
    total = part_ref[me].astype(jnp.float32)
    for step in range(1, members):
        copies[step - 1].wait()
        total = total + came[step].astype(jnp.float32)
    if not gather:
        out_ref[...] = (base_ref[...] + total).astype(out_ref.dtype)
        return
    out_ref[me] = total.astype(out_ref.dtype)
    copies = []
    for step in range(1, members):
        copies.append(
            pltpu.make_async_remote_copy(
                src_ref=out_ref.at[me],
                dst_ref=out_ref.at[me],
                send_sem=send_back.at[step],
                recv_sem=recv_back.at[step],
                device_id={"grp": peers[step]},
                device_id_type=pl.DeviceIdType.MESH,
            )
        )
        copies[-1].start()
    for copy in copies:
        copy.wait()


def sum_over_grp(parts, base=None):
    members, rows, share = parts.shape
    gather = base is None
    sems = [pltpu.SemaphoreType.DMA((members,))] * (4 if gather else 2)
    operands = (parts,) if gather else (parts, base)
    return pl.pallas_call(
        functools.partial(sum_body, members, gather),
        out_shape=jax.ShapeDtypeStruct(parts.shape if gather else (rows, share), jnp.bfloat16),
        in_specs=[pl.BlockSpec(memory_space=pltpu.VMEM)] * len(operands),
        out_specs=pl.BlockSpec(memory_space=pltpu.VMEM),
        scratch_shapes=[pltpu.VMEM(parts.shape, jnp.bfloat16)] + sems,
        compiler_params=pltpu.CompilerParams(
            collective_id=1 if gather else 2, has_side_effects=True
        ),
        name="sum_hidden" if gather else "sum_output",
    )(*operands)


def delta_body(
    steps,
    reqs,
    hidden_ref,
    input_ref,
    beta_ref,
    decay_down_ref,
    decay_up_ref,
    gate_down_ref,
    gate_up_ref,
    rate_ref,
    state_ref,
    output_ref,
    out_ref,
    kin,
    decay_low,
    gate_low,
    betas,
    total,
):
    turn = pl.program_id(0)
    sources, _, pair, _, _ = state_ref.shape
    each = hidden_ref.shape[0]
    pieces, _, share = out_ref.shape
    f32, bf16 = jnp.float32, jnp.bfloat16
    nt = (((1,), (1,)), ((), ()))

    @pl.when(turn == 0)
    def _():
        kin[...] = norm_rows(hidden_ref[...]).astype(bf16)
        rows = kin[...]
        decay_low[...] = jnp.dot(rows, decay_down_ref[...], preferred_element_type=f32).astype(bf16)
        gate_low[...] = jnp.dot(rows, gate_down_ref[...], preferred_element_type=f32).astype(bf16)
        betas[...] = jax.nn.sigmoid(jnp.dot(rows, beta_ref[...], preferred_element_type=f32))
        total[...] = jnp.zeros_like(total)

    rows = kin[...]
    query, key, value = [jnp.dot(rows, input_ref[i], preferred_element_type=f32) for i in range(3)]
    raw = jnp.dot(decay_low[...], decay_up_ref[...], preferred_element_type=f32)
    soft = jnp.maximum(raw, 0.0) + jnp.log1p(jnp.exp(-jnp.abs(raw)))
    decays = jnp.exp(-rate_ref[...] * soft)
    gate = jax.nn.sigmoid(jnp.dot(gate_low[...], gate_up_ref[...], preferred_element_type=f32))
    lane = lax.broadcasted_iota(jnp.int32, betas.shape, 1)
    owner_row = lax.rem(lax.broadcasted_iota(jnp.int32, (2 * steps * reqs, 1), 0), reqs)
    results = []
    for h in range(pair):
        cut = slice(h * DK, (h + 1) * DK)
        beta = jnp.sum(
            jnp.where(lane == turn * pair + h, betas[...], 0.0), axis=1, keepdims=True
        )
        units = (unit_rows(key[:, cut]), unit_rows(query[:, cut]) * DK ** (-0.5))
        at = [slice(t * reqs, (t + 1) * reqs) for t in range(steps)]
        keys = [units[0][a] for a in at]
        queries = [units[1][a] for a in at]
        decay = [decays[a, cut] for a in at]
        grown = [decay[0]]
        for t in range(1, steps):
            grown.append(grown[-1] * decay[t])
        looks = jnp.concatenate(
            [keys[t] * grown[t] for t in range(steps)]
            + [queries[t] * grown[t] for t in range(steps)],
            axis=0,
        ).astype(bf16)
        seen = jnp.zeros(looks.shape, f32)
        for r in range(reqs):
            state = state_ref[:, r, h].reshape(DV, DK)
            found = lax.dot_general(looks, state, nt, preferred_element_type=f32)
            seen = jnp.where(owner_row == r, found, seen)
        written = []
        reads = []
        for t in range(steps):
            if t:
                written = [(e, k * decay[t]) for e, k in written]
            err = value[at[t], cut] - seen[t * reqs : (t + 1) * reqs]
            for e, k in written:
                err = err - e * jnp.sum(k * keys[t], axis=1, keepdims=True)
            written.append((beta[at[t]] * err, keys[t]))
            read = seen[(steps + t) * reqs : (steps + t + 1) * reqs]
            for e, k in written:
                read = read + e * jnp.sum(k * queries[t], axis=1, keepdims=True)
            reads.append(norm_rows(read) * gate[at[t], cut])
        reads.append(jnp.zeros((each - steps * reqs, DV), f32))
        results.append(jnp.concatenate(reads, axis=0).astype(bf16))
    total[...] += jnp.dot(
        jnp.concatenate(results, axis=1), output_ref[...], preferred_element_type=f32
    )

    @pl.when(turn == pl.num_programs(0) - 1)
    def _():
        for p in range(pieces):
            out_ref[p] = total[:, p * share : (p + 1) * share].astype(out_ref.dtype)


def delta_steps(
    steps,
    reqs,
    pieces,
    hidden,
    kda_inputs,
    kda_beta,
    decay_down,
    decay_up,
    gate_down,
    gate_up,
    rate,
    states,
    kda_output,
):
    each, width = hidden.shape
    heads = kda_beta.shape[1]
    pair = 2
    sources, _, _, part, _ = states.shape
    whole = lambda h: (0, 0)
    wide = lambda h: (0, h)
    return pl.pallas_call(
        functools.partial(delta_body, steps, reqs),
        out_shape=jax.ShapeDtypeStruct((pieces, each, width // pieces), jnp.bfloat16),
        grid=(heads // pair,),
        in_specs=[
            pl.BlockSpec((each, width), whole),
            pl.BlockSpec((3, width, pair * DK), lambda h: (0, 0, h)),
            pl.BlockSpec((width, heads), whole),
            pl.BlockSpec(decay_down.shape, whole),
            pl.BlockSpec((decay_up.shape[0], pair * DK), wide),
            pl.BlockSpec(gate_down.shape, whole),
            pl.BlockSpec((gate_up.shape[0], pair * DV), wide),
            pl.BlockSpec((1, pair * DK), wide),
            pl.BlockSpec((sources, reqs, pair, part, DK), lambda h: (0, 0, h, 0, 0)),
            pl.BlockSpec((pair * DV, width), lambda h: (h, 0)),
        ],
        out_specs=pl.BlockSpec((pieces, each, width // pieces), lambda h: (0, 0, 0)),
        scratch_shapes=[
            pltpu.VMEM((each, width), jnp.bfloat16),
            pltpu.VMEM((each, decay_down.shape[1]), jnp.bfloat16),
            pltpu.VMEM((each, gate_down.shape[1]), jnp.bfloat16),
            pltpu.VMEM((each, heads), jnp.float32),
            pltpu.VMEM((each, width), jnp.float32),
        ],
        compiler_params=pltpu.CompilerParams(vmem_limit_bytes=40 * 1024 * 1024),
        name="delta_steps",
    )(
        hidden,
        kda_inputs,
        kda_beta,
        decay_down,
        decay_up,
        gate_down,
        gate_up,
        rate,
        states,
        kda_output,
    )


def shards(
    x_group,
    decode_input,
    prompt_len,
    latent_pages,
    slot_target,
    page_counts,
    kda_state,
    query_proj,
    latent_proj,
    key_expand,
    value_expand,
    mla_output,
    kda_inputs,
    kda_beta,
    decay_down,
    decay_up,
    gate_down,
    gate_up,
    decay_log,
    kda_output,
):
    f32, bf16 = jnp.float32, jnp.bfloat16
    seq_index = lax.axis_index("seq")
    grp_index = lax.axis_index("grp")
    owners = lax.axis_size("seq")
    heads = key_expand.shape[1] // NOPE
    width = x_group.shape[1]
    share = width // lax.axis_size("grp")
    col = grp_index * share
    steps, reqs, _ = decode_input.shape
    cap = slot_target.shape[2]
    n = steps * reqs

    dec_own = decode_input.reshape(n, width)
    group_rows = x_group.shape[0]
    rows_share = group_rows // lax.axis_size("grp")
    x_normed = norm_rows(x_group.astype(f32)).astype(bf16)
    own_normed = norm_rows(dec_own.astype(f32)).astype(bf16)
    own_place = (prompt_len[None, :] + jnp.arange(steps)[:, None]).reshape(n)
    share_normed = lax.dynamic_slice_in_dim(x_normed, grp_index * rows_share, rows_share, 0)
    share_place = seq_index * group_rows + grp_index * rows_share + jnp.arange(rows_share)
    latents = make_latent(
        jnp.concatenate([share_normed, own_normed]),
        latent_proj,
        jnp.concatenate([share_place, own_place]),
    )
    fresh = latents[rows_share:]
    each = -(-(n + 1) // 16) * 16
    numbers = jnp.concatenate(
        [prompt_len // PAGE, prompt_len % PAGE, page_counts[:, 0], slot_target.reshape(-1)]
    ).astype(bf16)
    numbers = jnp.pad(numbers, (0, width - numbers.shape[0]))[None]
    payload = jnp.concatenate(
        [own_normed, numbers, jnp.zeros((each - n - 1, width), bf16)], axis=0
    )
    members = lax.axis_size("grp")
    block = lax.dynamic_slice_in_dim(payload, col, share, 1).reshape(-1, LAT + ROPE)
    blocks = gather_blocks(
        jnp.concatenate([latents[:rows_share], block]), owners, members
    )
    shard_rows = blocks[:, :, :rows_share].reshape(-1, LAT + ROPE)
    dec_all = (
        blocks[:, :, rows_share:]
        .reshape(owners, members, each, share)
        .transpose(0, 2, 1, 3)
        .reshape(owners * each, width)
    )
    numbers = dec_all.reshape(owners, each, width)[:, n, : 2 * reqs + owners + owners * cap]
    ints = numbers.astype(jnp.int32)
    lens_all = ints[:, :reqs] * PAGE + ints[:, reqs : 2 * reqs]
    counts = lax.dynamic_slice_in_dim(ints, 2 * reqs + seq_index, 1, 1)
    targets = lax.dynamic_slice_in_dim(ints, 2 * reqs + owners + seq_index * cap, cap, 1)

    states = kda_state.astype(bf16).reshape((owners, reqs) + kda_state.shape[1:])
    states = lax.all_to_all(states, "seq", split_axis=0, concat_axis=0, tiled=True)

    position = seq_index * group_rows + jnp.arange(group_rows)
    dec_place = (lens_all[:, None, :] + jnp.arange(each // reqs)[None, :, None]).reshape(-1)
    place = jnp.concatenate([position, dec_place]).astype(f32)
    half = ROPE // 2
    angles = place[:, None] * jnp.exp(-jnp.log(10000.0) * jnp.arange(half, dtype=f32) / half)
    cosine, sine = jnp.cos(angles), jnp.sin(angles)
    queries, qc = make_queries(
        jnp.concatenate([x_normed, dec_all]),
        group_rows,
        owners,
        query_proj,
        key_expand,
        jnp.concatenate([cosine, cosine], axis=1),
        jnp.concatenate([-sine, sine], axis=1),
    )

    pages = latent_pages.reshape(owners, cap * PAGE, LAT + ROPE)
    token = (targets % MAXP)[..., None] * PAGE + jnp.arange(PAGE)
    holder = targets // MAXP
    length = jnp.sum(
        jnp.where(holder[..., None] == jnp.arange(reqs), lens_all[:, None, :], 0), axis=-1
    )
    live = (jnp.arange(cap)[None, :] < counts)[..., None] & (token < length[..., None])
    holders = jnp.where(live, holder[..., None], -1).reshape(owners, 1, cap * PAGE)
    sent = attend_pages(reqs, qc, pages, holders, value_expand)
    sent, shard_rows = lax.optimization_barrier((sent, shard_rows))
    came = lax.all_to_all(
        sent.reshape(owners, each, -1), "seq", split_axis=0, concat_axis=0, tiled=True
    )

    heads_out = prefill_attend(seq_index, queries, shard_rows, key_expand, value_expand)
    prefill_part = jnp.dot(heads_out, mla_output, preferred_element_type=f32)
    came, prefill_part = lax.optimization_barrier((came, prefill_part))
    attended = lax.psum_scatter(
        prefill_part.astype(bf16), "grp", scatter_dimension=1, tiled=True
    )

    pieces = lax.axis_size("grp")
    fresh = jnp.pad(fresh, ((0, each - n), (0, 0)))
    own_query = lax.dynamic_index_in_dim(qc, seq_index, 0, keepdims=False)
    own_query = own_query.reshape(heads, each, LAT + ROPE)
    mla_parts = merge_parts(
        reqs, n, pieces, came, own_query, fresh, value_expand, mla_output
    )
    mla_total = sum_over_grp(mla_parts)
    dec_rows = jnp.pad(dec_own, ((0, each - n), (0, 0))).astype(f32)
    hidden = dec_rows + mla_total.transpose(1, 0, 2).reshape(each, width).astype(f32)

    kda_parts = delta_steps(
        steps,
        reqs,
        pieces,
        hidden,
        kda_inputs.transpose(1, 0, 2),
        kda_beta,
        decay_down,
        decay_up,
        gate_down,
        gate_up,
        jnp.repeat(jnp.exp(decay_log), DK)[None],
        states,
        kda_output,
    )
    kda_parts, attended = lax.optimization_barrier((kda_parts, attended))
    decode_out = sum_over_grp(kda_parts, lax.dynamic_slice_in_dim(hidden, col, share, 1))
    prefill_out = (
        lax.dynamic_slice_in_dim(x_group, col, share, 1).astype(f32) + attended.astype(f32)
    ).astype(bf16)
    return (prefill_out, decode_out[:n].reshape(steps, reqs, share))


def solution(mesh):
    in_specs = (
        P("seq", None),
        P(None, "seq", None),
        P("seq"),
        P("seq", None, None, None, None),
        P(None, "seq", None),
        P(None, "seq"),
        P(None, "grp", "seq", None),
        P(None, "grp"),
        P(),
        P(None, "grp"),
        P(None, "grp"),
        P("grp", None),
        P(None, None, "grp"),
        P(None, "grp"),
        P(),
        P(None, "grp"),
        P(),
        P(None, "grp"),
        P("grp"),
        P("grp", None),
    )
    out_specs = (P("seq", "grp"), P(None, "seq", "grp"))
    return jax.shard_map(shards, mesh=mesh, in_specs=in_specs, out_specs=out_specs, check_vma=False)
```

```python
import functools

import jax
import jax.numpy as jnp
from jax import lax
from jax.experimental import pallas as pl
from jax.experimental.pallas import tpu as pltpu
from jax.sharding import PartitionSpec as P

LAT = 512
ROPE = 64
NOPE = 128
VH = 128
DK = 128
DV = 128
PAGE = 64
MAXP = 12


epsilon = 1e-06
masked_score = -1e30


def norm_rows(values):
    return values * lax.rsqrt(jnp.mean(values * values, axis=-1, keepdims=True) + epsilon)


def unit_rows(values):
    return values * lax.rsqrt(jnp.sum(values * values, axis=-1, keepdims=True) + epsilon)


def prefill_body(
    place_ref,
    query_ref,
    rows_ref,
    key_ref,
    value_ref,
    weight_ref,
    out_ref,
    peak,
    total,
    mixed,
    result,
):
    pair, group_rows, _ = query_ref.shape
    nt = (((1,), (1,)), ((), ()))
    factor = (NOPE + ROPE) ** (-0.5) * 1.4426950408889634
    own = place_ref[0]

    def chunk(index, first):
        rows = rows_ref[pl.ds(pl.multiple_of(index * group_rows, group_rows), group_rows), :]
        latent = rows[:, :LAT]
        keys = jnp.dot(latent, key_ref[...], preferred_element_type=jnp.float32)
        keys = keys.astype(jnp.bfloat16)
        values = lax.dot_general(value_ref[...], latent, nt, preferred_element_type=jnp.float32)
        values = values.astype(jnp.bfloat16)
        for h in range(pair):
            full = jnp.concatenate([keys[:, h * NOPE : (h + 1) * NOPE], rows[:, LAT:]], axis=1)
            scores = lax.dot_general(full, query_ref[h], nt, preferred_element_type=jnp.float32)
            if first:
                key_at = lax.broadcasted_iota(jnp.int32, scores.shape, 0)
                query_at = lax.broadcasted_iota(jnp.int32, scores.shape, 1)
                scores = jnp.where(key_at <= query_at, scores, masked_score)
            top = jnp.max(scores, axis=0, keepdims=True)
            if not first:
                top = jnp.maximum(top, peak[h])
            weights = jnp.exp2((scores - top) * factor)
            summed = jnp.sum(weights, axis=0, keepdims=True)
            added = jnp.dot(
                values[h * VH : (h + 1) * VH],
                weights.astype(jnp.bfloat16),
                preferred_element_type=jnp.float32,
            )
            if first:
                total[h] = summed
                mixed[h] = added
            else:
                shrink = jnp.exp2((peak[h] - top) * factor)
                total[h] = total[h] * shrink + summed
                mixed[h] = mixed[h] * shrink + added
            peak[h] = top

    chunk(own, True)

    @pl.loop(0, own)
    def _(index):
        chunk(index, False)

    attended = jnp.concatenate(
        [(mixed[h] / total[h]).T.astype(jnp.bfloat16) for h in range(pair)], axis=1
    )
    pieces, _, share = out_ref.shape
    turn = pl.program_id(0)

    @pl.when(turn == 0)
    def _():
        result[...] = jnp.zeros_like(result)

    width = result.shape[1]
    step = width // 3 if width % 384 == 0 else width
    for at in range(0, width, step):
        cut = slice(at, at + step)
        result[:, cut] += jnp.dot(
            attended, weight_ref[:, cut], preferred_element_type=jnp.float32
        )

    @pl.when(turn == pl.num_programs(0) - 1)
    def _():
        for p in range(pieces):
            out_ref[p] = result[:, p * share : (p + 1) * share].astype(out_ref.dtype)


def prefill_attend(seq_index, pieces, queries, rows, key_expand, value_expand, mla_output):
    heads, group_rows, _ = queries.shape
    pair = 4 if heads % 4 == 0 else 2
    row_count = rows.shape[0]
    width = mla_output.shape[1]
    return pl.pallas_call(
        prefill_body,
        out_shape=jax.ShapeDtypeStruct((pieces, group_rows, width // pieces), jnp.bfloat16),
        grid_spec=pltpu.PrefetchScalarGridSpec(
            num_scalar_prefetch=1,
            grid=(heads // pair,),
            in_specs=[
                pl.BlockSpec((pair, group_rows, NOPE + ROPE), lambda h, p: (h, 0, 0)),
                pl.BlockSpec((row_count, LAT + ROPE), lambda h, p: (0, 0)),
                pl.BlockSpec((LAT, pair * NOPE), lambda h, p: (0, h)),
                pl.BlockSpec((pair * VH, LAT), lambda h, p: (h, 0)),
                pl.BlockSpec((pair * VH, width), lambda h, p: (h, 0)),
            ],
            out_specs=pl.BlockSpec((pieces, group_rows, width // pieces), lambda h, p: (0, 0, 0)),
            scratch_shapes=[
                pltpu.VMEM((pair, 1, group_rows), jnp.float32),
                pltpu.VMEM((pair, 1, group_rows), jnp.float32),
                pltpu.VMEM((pair, VH, group_rows), jnp.float32),
                pltpu.VMEM((group_rows, width), jnp.float32),
            ],
        ),
        compiler_params=pltpu.CompilerParams(vmem_limit_bytes=56 * 1024 * 1024),
        cost_estimate=pl.CostEstimate(
            flops=2 * heads * group_rows * row_count * 4 * NOPE,
            bytes_accessed=row_count * (LAT + ROPE) * 4,
            transcendentals=heads * group_rows * row_count,
        ),
        name="prefill_attend",
    )(
        seq_index.reshape(1).astype(jnp.int32),
        queries,
        rows,
        key_expand,
        value_expand.T,
        mla_output,
    )


def prepare_body(count, rows_ref, weight_ref, cos_ref, sin_ref, own_ref, block_ref, fresh_ref):
    rows = norm_rows(rows_ref[...].astype(jnp.float32)).astype(jnp.bfloat16)
    nt = (((1,), (1,)), ((), ()))
    projected = lax.dot_general(rows, weight_ref[...], nt, preferred_element_type=jnp.float32)
    rope = projected[:, LAT:]
    turned = jnp.concatenate([rope[:, ROPE // 2 :], rope[:, : ROPE // 2]], axis=1)
    rope = rope * cos_ref[...] + turned * sin_ref[...]
    latents = jnp.concatenate([norm_rows(projected[:, :LAT]), rope], axis=1).astype(jnp.bfloat16)
    block_ref[:count] = latents[:count]
    block_ref[count:] = own_ref[...]
    fresh_ref[...] = latents[count:]


def prepare(count, rows, latent_proj, cosine, sine, own):
    depth = latent_proj.shape[1]
    return pl.pallas_call(
        functools.partial(prepare_body, count),
        out_shape=(
            jax.ShapeDtypeStruct((count + own.shape[0], depth), jnp.bfloat16),
            jax.ShapeDtypeStruct((rows.shape[0] - count, depth), jnp.bfloat16),
        ),
        in_specs=[pl.BlockSpec(memory_space=pltpu.VMEM)] * 5,
        out_specs=[pl.BlockSpec(memory_space=pltpu.VMEM)] * 2,
        compiler_params=pltpu.CompilerParams(vmem_limit_bytes=32 * 1024 * 1024),
        name="prepare",
    )(rows, latent_proj.T, cosine, sine, own)


def turns(place):
    half = ROPE // 2
    frequency = jnp.exp(-jnp.log(10000.0) * jnp.arange(half, dtype=jnp.float32) / half)
    angles = place.astype(jnp.float32)[:, None] * frequency
    cosine, sine = jnp.cos(angles), jnp.sin(angles)
    return (
        jnp.concatenate([cosine, cosine], axis=1),
        jnp.concatenate([-sine, sine], axis=1),
    )


def gather_body(sizes, own_ref, all_ref, *sems):
    zs, ys, xs, cs = sizes
    z_send, z_recv, y_send, y_recv, x_send, x_recv, c_send, c_recv, local_sem = sems
    seq_at, grp_at = lax.axis_index("seq"), lax.axis_index("grp")
    z, y = seq_at // ys, lax.rem(seq_at, ys)
    x, c = grp_at // cs, lax.rem(grp_at, cs)

    def seq_of(dz, dy):
        return lax.rem(z + dz + zs, zs) * ys + lax.rem(y + dy + ys, ys)

    def grp_of(dx, dc):
        return lax.rem(x + dx + xs, xs) * cs + lax.rem(c + dc + cs, cs)

    z_peers = [{"seq": seq_of(d, 0)} for d in range(zs)]
    y_peers = [{"seq": seq_of(0, d)} for d in range(ys)]
    x_peers = [{"grp": grp_of(d, 0)} for d in range(xs)]
    c_peers = [{"grp": grp_of(0, d)} for d in range(cs)]
    peers = z_peers[1:] + y_peers[1:] + x_peers[1:] + c_peers[1:]
    barrier = pltpu.get_barrier_semaphore()
    for peer in peers:
        pl.semaphore_signal(
            barrier, inc=1, device_id=peer, device_id_type=pl.DeviceIdType.MESH
        )
    pl.semaphore_wait(barrier, len(peers))

    started = []

    def push(back, peer, send, recv):
        dz, dy, dx = back
        place = all_ref.at[seq_of(-dz, -dy), grp_of(-dx, 0)]
        copy = pltpu.make_async_remote_copy(
            src_ref=place if any(back) else own_ref,
            dst_ref=place,
            send_sem=send,
            recv_sem=recv,
            device_id=peer,
            device_id_type=pl.DeviceIdType.MESH,
        )
        copy.start()
        started.append(copy)
        return copy

    by_z, by_y, by_x, by_c = {}, {}, {}, {}

    def across(dz, dy):
        for d in range(1, xs):
            at = (d, dz, dy)
            by_x[at] = push((dz, dy, 0), x_peers[d], x_send.at[at], x_recv.at[at])
        to_core(0, dz, dy)

    def to_core(dx, dz, dy):
        for d in range(1, cs):
            at = (dx, dz, dy)
            by_c[(d,) + at] = push((dz, dy, dx), c_peers[d], c_send.at[at], c_recv.at[at])

    def along(dz):
        for d in range(1, ys):
            by_y[d, dz] = push((dz, 0, 0), y_peers[d], y_send.at[d, dz], y_recv.at[d, dz])
        across(dz, 0)

    local = pltpu.make_async_copy(own_ref, all_ref.at[seq_at, grp_at], local_sem)
    local.start()
    for d in range(1, zs):
        by_z[d] = push((0, 0, 0), z_peers[d], z_send.at[d], z_recv.at[d])
    along(0)
    for dz in range(1, zs):
        by_z[dz].wait_recv()
        along(dz)
    for dz in range(zs):
        for dy in range(1, ys):
            by_y[dy, dz].wait_recv()
            across(dz, dy)
    for at in list(by_x):
        by_x[at].wait_recv()
        to_core(*at)
    for copy in by_c.values():
        copy.wait_recv()
    local.wait()
    for copy in started:
        copy.wait_send()


def gather_blocks(own, owners, members):
    rows, width = own.shape
    cs = 2 if members % 2 == 0 else 1
    zs = 4 if owners % 4 == 0 else owners
    sizes = (zs, owners // zs, members // cs, cs)
    zs, ys, xs, cs = sizes
    shapes = [(zs,), (ys, zs), (xs, zs, ys), (xs, zs, ys)]
    sems = [pltpu.SemaphoreType.DMA(shape) for shape in shapes for _ in range(2)]
    return pl.pallas_call(
        functools.partial(gather_body, sizes),
        out_shape=jax.ShapeDtypeStruct((owners, members, rows, width), own.dtype),
        in_specs=[pl.BlockSpec(memory_space=pltpu.VMEM)],
        out_specs=pl.BlockSpec(memory_space=pltpu.VMEM),
        scratch_shapes=sems + [pltpu.SemaphoreType.DMA],
        compiler_params=pltpu.CompilerParams(
            collective_id=0, has_side_effects=True, vmem_limit_bytes=56 * 1024 * 1024
        ),
        name="gather_blocks",
    )(own)


def query_body(
    group_ref, dec_ref, weight_ref, key_ref, cos_ref, sin_ref, prefill_ref, decode_ref, rows_ref
):
    pair, group_rows, _ = prefill_ref.shape
    owners, slab, _ = decode_ref.shape
    each = slab // pair
    nt = (((1,), (1,)), ((), ()))

    @pl.when(pl.program_id(0) == 0)
    def _():
        half = dec_ref.shape[0] // 2
        rows_ref[:group_rows] = norm_rows(group_ref[...].astype(jnp.float32)).astype(jnp.bfloat16)
        for at in range(0, 2 * half, half):
            rows_ref[group_rows + at : group_rows + at + half] = norm_rows(
                dec_ref[at : at + half].astype(jnp.float32)
            ).astype(jnp.bfloat16)

    projected = jnp.dot(rows_ref[...], weight_ref[...], preferred_element_type=jnp.float32)
    for h in range(pair):
        start = h * (NOPE + ROPE)
        nope = projected[:, start : start + NOPE].astype(jnp.bfloat16)
        rope = projected[:, start + NOPE : start + NOPE + ROPE]
        turned = jnp.concatenate([rope[:, ROPE // 2 :], rope[:, : ROPE // 2]], axis=1)
        rope = (rope * cos_ref[...] + turned * sin_ref[...]).astype(jnp.bfloat16)
        prefill_ref[h] = jnp.concatenate([nope[:group_rows], rope[:group_rows]], axis=1)
        latent = lax.dot_general(
            nope[group_rows:],
            key_ref[:, h * NOPE : (h + 1) * NOPE],
            nt,
            preferred_element_type=jnp.float32,
        ).astype(jnp.bfloat16)
        full = jnp.concatenate([latent, rope[group_rows:]], axis=1)
        decode_ref[:, h * each : (h + 1) * each, :] = full.reshape(owners, each, LAT + ROPE)


def make_queries(group, dec, owners, query_proj, key_expand, cosine, sine):
    pair = 2
    group_rows, width = group.shape
    total = group_rows + dec.shape[0]
    heads = key_expand.shape[1] // NOPE
    each = (total - group_rows) // owners
    return pl.pallas_call(
        query_body,
        out_shape=(
            jax.ShapeDtypeStruct((heads, group_rows, NOPE + ROPE), jnp.bfloat16),
            jax.ShapeDtypeStruct((owners, heads * each, LAT + ROPE), jnp.bfloat16),
        ),
        grid=(heads // pair,),
        in_specs=[
            pl.BlockSpec(group.shape, lambda h: (0, 0)),
            pl.BlockSpec(dec.shape, lambda h: (0, 0)),
            pl.BlockSpec((width, pair * (NOPE + ROPE)), lambda h: (0, h)),
            pl.BlockSpec((LAT, pair * NOPE), lambda h: (0, h)),
            pl.BlockSpec((total, ROPE), lambda h: (0, 0)),
            pl.BlockSpec((total, ROPE), lambda h: (0, 0)),
        ],
        out_specs=(
            pl.BlockSpec((pair, group_rows, NOPE + ROPE), lambda h: (h, 0, 0)),
            pl.BlockSpec((owners, pair * each, LAT + ROPE), lambda h: (0, h, 0)),
        ),
        scratch_shapes=[pltpu.VMEM((total, width), jnp.bfloat16)],
        compiler_params=pltpu.CompilerParams(vmem_limit_bytes=56 * 1024 * 1024),
        cost_estimate=pl.CostEstimate(
            flops=2 * total * width * query_proj.shape[1],
            bytes_accessed=2 * width * (query_proj.shape[1] + total),
            transcendentals=0,
        ),
        name="make_queries",
    )(group, dec, query_proj, key_expand, cosine, sine)


def page_body(reqs, query_ref, page_ref, holder_ref, value_ref, out_ref, parts, logs):
    owner = pl.program_id(0)
    heads, _, _ = parts.shape
    rows = query_ref.shape[1]
    each = rows // heads
    keys = page_ref[0]
    nt = (((1,), (1,)), ((), ()))
    scores = lax.dot_general(query_ref[0], keys, nt, preferred_element_type=jnp.float32)
    request = lax.rem(lax.broadcasted_iota(jnp.int32, (rows, 1), 0), reqs)
    live = holder_ref[0] == request
    scores = jnp.where(live, scores * (NOPE + ROPE) ** (-0.5), masked_score)
    highest = jnp.max(scores, axis=1, keepdims=True)
    weights = jnp.where(live, jnp.exp(scores - highest), 0.0)
    totals = jnp.sum(weights, axis=1, keepdims=True)
    safe = jnp.maximum(totals, 1e-30)
    summed = jnp.dot(weights.astype(jnp.bfloat16), keys[:, :LAT], preferred_element_type=jnp.float32)
    summed = (summed / safe).astype(jnp.bfloat16)
    place = pl.ds(pl.multiple_of(owner * each, each), each)
    parts[:, place, :] = summed.reshape(heads, each, LAT)
    log = jnp.where(totals > 0, highest + jnp.log(safe), masked_score)
    logs[:, place, :] = log.reshape(heads, each, 1)

    @pl.when(owner == pl.num_programs(0) - 1)
    def _():
        lane = lax.broadcasted_iota(jnp.int32, (parts.shape[1], 128), 1)
        tail = jnp.zeros((parts.shape[1], 128), jnp.float32)
        for h in range(heads):
            out_ref[:, h * VH : (h + 1) * VH] = jnp.dot(
                parts[h], value_ref[:, h * VH : (h + 1) * VH], preferred_element_type=jnp.float32
            ).astype(out_ref.dtype)
            high = logs[h].astype(jnp.bfloat16).astype(jnp.float32)
            tail = jnp.where(lane == h, high, tail)
            tail = jnp.where(lane == heads + h, logs[h] - high, tail)
        out_ref[:, heads * VH :] = tail.astype(out_ref.dtype)


def attend_pages(reqs, queries, pages, holders, value_expand):
    owners, rows, depth = queries.shape
    heads = value_expand.shape[1] // VH
    keys = pages.shape[1]
    total = owners * rows // heads
    return pl.pallas_call(
        functools.partial(page_body, reqs),
        out_shape=jax.ShapeDtypeStruct((total, heads * VH + 128), jnp.bfloat16),
        grid=(owners,),
        in_specs=[
            pl.BlockSpec((1, rows, depth), lambda o: (o, 0, 0)),
            pl.BlockSpec((1, keys, depth), lambda o: (o, 0, 0)),
            pl.BlockSpec((1, 1, keys), lambda o: (o, 0, 0)),
            pl.BlockSpec(value_expand.shape, lambda o: (0, 0)),
        ],
        out_specs=pl.BlockSpec((total, heads * VH + 128), lambda o: (0, 0)),
        scratch_shapes=[
            pltpu.VMEM((heads, total, LAT), jnp.bfloat16),
            pltpu.VMEM((heads, total, 1), jnp.float32),
        ],
        compiler_params=pltpu.CompilerParams(vmem_limit_bytes=56 * 1024 * 1024),
        cost_estimate=pl.CostEstimate(
            flops=4 * owners * rows * keys * depth,
            bytes_accessed=2 * owners * keys * depth,
            transcendentals=owners * rows * keys,
        ),
        name="attend_pages",
    )(queries, pages, holders, value_expand)


def merge_body(reqs, count, came_ref, query_ref, fresh_ref, value_ref, weight_ref, out_ref):
    owners, each, _ = came_ref.shape
    heads = query_ref.shape[0]
    pieces, _, share = out_ref.shape
    nt = (((1,), (1,)), ((), ()))
    fresh = fresh_ref[...]
    values = jnp.dot(fresh[:, :LAT], value_ref[...], preferred_element_type=jnp.float32)
    values = values.astype(jnp.bfloat16)
    row = lax.broadcasted_iota(jnp.int32, (each, each), 0)
    col = lax.broadcasted_iota(jnp.int32, (each, each), 1)
    live = (lax.rem(row, reqs) == lax.rem(col, reqs)) & (col <= row) & (col < count)
    logs = [came_ref[s, :, heads * VH :].astype(jnp.float32) for s in range(owners)]
    results = []
    for h in range(heads):
        scores = lax.dot_general(query_ref[h], fresh, nt, preferred_element_type=jnp.float32)
        scores = jnp.where(live, scores * (NOPE + ROPE) ** (-0.5), masked_score)
        log = [g[:, h : h + 1] + g[:, heads + h : heads + h + 1] for g in logs]
        top = jnp.max(scores, axis=1, keepdims=True)
        for one in log:
            top = jnp.maximum(top, one)
        weights = jnp.where(live, jnp.exp(scores - top), 0.0)
        total = jnp.sum(weights, axis=1, keepdims=True)
        cut = slice(h * VH, (h + 1) * VH)
        mixed = jnp.dot(
            weights.astype(jnp.bfloat16), values[:, cut], preferred_element_type=jnp.float32
        )
        for s in range(owners):
            factor = jnp.exp(log[s] - top)
            total = total + factor
            mixed = mixed + factor * came_ref[s, :, cut].astype(jnp.float32)
        results.append((mixed / total).astype(jnp.bfloat16))
    part = jnp.dot(
        jnp.concatenate(results, axis=1), weight_ref[...], preferred_element_type=jnp.float32
    )
    for p in range(pieces):
        out_ref[p] = part[:, p * share : (p + 1) * share].astype(out_ref.dtype)


def merge_parts(reqs, count, pieces, came, queries, fresh, value_expand, mla_output):
    each = came.shape[1]
    share = mla_output.shape[1] // pieces
    return pl.pallas_call(
        functools.partial(merge_body, reqs, count),
        out_shape=jax.ShapeDtypeStruct((pieces, each, share), jnp.bfloat16),
        in_specs=[pl.BlockSpec(memory_space=pltpu.VMEM)] * 5,
        out_specs=pl.BlockSpec(memory_space=pltpu.VMEM),
        compiler_params=pltpu.CompilerParams(vmem_limit_bytes=56 * 1024 * 1024),
        name="merge_parts",
    )(came, queries, fresh, value_expand, mla_output)


def sum_body(members, gather, part_ref, *refs):
    if gather:
        out_ref, came, send_sem, recv_sem, send_back, recv_back = refs
    else:
        mla_ref, dec_ref, out_ref, came, send_sem, recv_sem = refs
    me = lax.axis_index("grp")
    peers = [lax.rem(me + step, members) for step in range(members)]
    barrier = pltpu.get_barrier_semaphore()
    for peer in peers[1:]:
        pl.semaphore_signal(
            barrier, inc=1, device_id={"grp": peer}, device_id_type=pl.DeviceIdType.MESH
        )
    pl.semaphore_wait(barrier, members - 1)
    copies = []
    for step in range(1, members):
        copies.append(
            pltpu.make_async_remote_copy(
                src_ref=part_ref.at[peers[step]],
                dst_ref=came.at[step],
                send_sem=send_sem.at[step],
                recv_sem=recv_sem.at[step],
                device_id={"grp": peers[step]},
                device_id_type=pl.DeviceIdType.MESH,
            )
        )
        copies[-1].start()
    total = part_ref[me].astype(jnp.float32)
    for step in range(1, members):
        copies[step - 1].wait()
        total = total + came[step].astype(jnp.float32)
    if not gather:
        hidden = dec_ref[...].astype(jnp.float32) + mla_ref[me].astype(jnp.float32)
        out_ref[...] = (hidden + total).astype(out_ref.dtype)
        return
    out_ref[me] = total.astype(out_ref.dtype)
    copies = []
    for step in range(1, members):
        copies.append(
            pltpu.make_async_remote_copy(
                src_ref=out_ref.at[me],
                dst_ref=out_ref.at[me],
                send_sem=send_back.at[step],
                recv_sem=recv_back.at[step],
                device_id={"grp": peers[step]},
                device_id_type=pl.DeviceIdType.MESH,
            )
        )
        copies[-1].start()
    for copy in copies:
        copy.wait()


def sum_over_grp(parts, *base):
    members, rows, share = parts.shape
    gather = not base
    sems = [pltpu.SemaphoreType.DMA((members,))] * (4 if gather else 2)
    operands = (parts,) + base
    return pl.pallas_call(
        functools.partial(sum_body, members, gather),
        out_shape=jax.ShapeDtypeStruct(parts.shape if gather else (rows, share), jnp.bfloat16),
        in_specs=[pl.BlockSpec(memory_space=pltpu.VMEM)] * len(operands),
        out_specs=pl.BlockSpec(memory_space=pltpu.VMEM),
        scratch_shapes=[pltpu.VMEM(parts.shape, jnp.bfloat16)] + sems,
        compiler_params=pltpu.CompilerParams(
            collective_id=1 if gather else 2, has_side_effects=True
        ),
        name="sum_hidden" if gather else "sum_output",
    )(*operands)


def delta_body(
    steps,
    reqs,
    mla_ref,
    dec_ref,
    input_ref,
    beta_ref,
    decay_down_ref,
    decay_up_ref,
    gate_down_ref,
    gate_up_ref,
    rate_ref,
    state_ref,
    output_ref,
    out_ref,
    kin,
    decay_low,
    gate_low,
    betas,
    total,
):
    turn = pl.program_id(0)
    sources, _, pair, _, _ = state_ref.shape
    each = dec_ref.shape[0]
    pieces, _, share = out_ref.shape
    f32, bf16 = jnp.float32, jnp.bfloat16
    nt = (((1,), (1,)), ((), ()))

    @pl.when(turn == 0)
    def _():
        added = jnp.concatenate([mla_ref[p].astype(f32) for p in range(pieces)], axis=1)
        kin[...] = norm_rows(dec_ref[...].astype(f32) + added).astype(bf16)
        rows = kin[...]
        decay_low[...] = jnp.dot(rows, decay_down_ref[...], preferred_element_type=f32).astype(bf16)
        gate_low[...] = jnp.dot(rows, gate_down_ref[...], preferred_element_type=f32).astype(bf16)
        betas[...] = jax.nn.sigmoid(
            lax.dot_general(rows, beta_ref[...], nt, preferred_element_type=f32)
        )
        total[...] = jnp.zeros_like(total)

    rows = kin[...]
    query, key, value = [jnp.dot(rows, input_ref[i], preferred_element_type=f32) for i in range(3)]
    raw = jnp.dot(decay_low[...], decay_up_ref[...], preferred_element_type=f32)
    soft = jnp.maximum(raw, 0.0) + jnp.log1p(jnp.exp(-jnp.abs(raw)))
    decays = jnp.exp(-rate_ref[...] * soft)
    gate = jax.nn.sigmoid(jnp.dot(gate_low[...], gate_up_ref[...], preferred_element_type=f32))
    lane = lax.broadcasted_iota(jnp.int32, betas.shape, 1)
    owner_row = lax.rem(lax.broadcasted_iota(jnp.int32, (2 * steps * reqs, 1), 0), reqs)
    results = []
    for h in range(pair):
        cut = slice(h * DK, (h + 1) * DK)
        beta = jnp.sum(
            jnp.where(lane == turn * pair + h, betas[...], 0.0), axis=1, keepdims=True
        )
        units = (unit_rows(key[:, cut]), unit_rows(query[:, cut]) * DK ** (-0.5))
        at = [slice(t * reqs, (t + 1) * reqs) for t in range(steps)]
        keys = [units[0][a] for a in at]
        queries = [units[1][a] for a in at]
        decay = [decays[a, cut] for a in at]
        grown = [decay[0]]
        for t in range(1, steps):
            grown.append(grown[-1] * decay[t])
        looks = jnp.concatenate(
            [keys[t] * grown[t] for t in range(steps)]
            + [queries[t] * grown[t] for t in range(steps)],
            axis=0,
        ).astype(bf16)
        seen = jnp.zeros(looks.shape, f32)
        for r in range(reqs):
            state = state_ref[:, r, h].reshape(DV, DK)
            found = lax.dot_general(looks, state, nt, preferred_element_type=f32)
            seen = jnp.where(owner_row == r, found, seen)
        written = []
        reads = []
        for t in range(steps):
            if t:
                written = [(e, k * decay[t]) for e, k in written]
            err = value[at[t], cut] - seen[t * reqs : (t + 1) * reqs]
            for e, k in written:
                err = err - e * jnp.sum(k * keys[t], axis=1, keepdims=True)
            written.append((beta[at[t]] * err, keys[t]))
            read = seen[(steps + t) * reqs : (steps + t + 1) * reqs]
            for e, k in written:
                read = read + e * jnp.sum(k * queries[t], axis=1, keepdims=True)
            reads.append(norm_rows(read) * gate[at[t], cut])
        reads.append(jnp.zeros((each - steps * reqs, DV), f32))
        results.append(jnp.concatenate(reads, axis=0).astype(bf16))
    total[...] += jnp.dot(
        jnp.concatenate(results, axis=1), output_ref[...], preferred_element_type=f32
    )

    @pl.when(turn == pl.num_programs(0) - 1)
    def _():
        for p in range(pieces):
            out_ref[p] = total[:, p * share : (p + 1) * share].astype(out_ref.dtype)


def delta_steps(
    steps,
    reqs,
    mla_total,
    dec_rows,
    kda_inputs,
    kda_beta,
    decay_down,
    decay_up,
    gate_down,
    gate_up,
    rate,
    states,
    kda_output,
):
    each, width = dec_rows.shape
    pieces = mla_total.shape[0]
    heads = kda_beta.shape[1]
    pair = 2
    sources, _, _, part, _ = states.shape
    whole = lambda h: (0, 0)
    wide = lambda h: (0, h)
    return pl.pallas_call(
        functools.partial(delta_body, steps, reqs),
        out_shape=jax.ShapeDtypeStruct((pieces, each, width // pieces), jnp.bfloat16),
        grid=(heads // pair,),
        in_specs=[
            pl.BlockSpec(mla_total.shape, lambda h: (0, 0, 0)),
            pl.BlockSpec((each, width), whole),
            pl.BlockSpec((3, width, pair * DK), lambda h: (0, 0, h)),
            pl.BlockSpec((heads, width), whole),
            pl.BlockSpec(decay_down.shape, whole),
            pl.BlockSpec((decay_up.shape[0], pair * DK), wide),
            pl.BlockSpec(gate_down.shape, whole),
            pl.BlockSpec((gate_up.shape[0], pair * DV), wide),
            pl.BlockSpec((1, pair * DK), wide),
            pl.BlockSpec((sources, reqs, pair, part, DK), lambda h: (0, 0, h, 0, 0)),
            pl.BlockSpec((pair * DV, width), lambda h: (h, 0)),
        ],
        out_specs=pl.BlockSpec((pieces, each, width // pieces), lambda h: (0, 0, 0)),
        scratch_shapes=[
            pltpu.VMEM((each, width), jnp.bfloat16),
            pltpu.VMEM((each, decay_down.shape[1]), jnp.bfloat16),
            pltpu.VMEM((each, gate_down.shape[1]), jnp.bfloat16),
            pltpu.VMEM((each, heads), jnp.float32),
            pltpu.VMEM((each, width), jnp.float32),
        ],
        compiler_params=pltpu.CompilerParams(vmem_limit_bytes=56 * 1024 * 1024),
        name="delta_steps",
    )(
        mla_total,
        dec_rows,
        kda_inputs,
        kda_beta.T,
        decay_down,
        decay_up,
        gate_down,
        gate_up,
        rate,
        states,
        kda_output,
    )


def shards(
    x_group,
    decode_input,
    prompt_len,
    latent_pages,
    slot_target,
    page_counts,
    kda_state,
    query_proj,
    latent_proj,
    key_expand,
    value_expand,
    mla_output,
    kda_inputs,
    kda_beta,
    decay_down,
    decay_up,
    gate_down,
    gate_up,
    decay_log,
    kda_output,
):
    f32, bf16 = jnp.float32, jnp.bfloat16
    seq_index = lax.axis_index("seq")
    grp_index = lax.axis_index("grp")
    owners = lax.axis_size("seq")
    heads = key_expand.shape[1] // NOPE
    width = x_group.shape[1]
    share = width // lax.axis_size("grp")
    col = grp_index * share
    steps, reqs, _ = decode_input.shape
    cap = slot_target.shape[2]
    n = steps * reqs

    dec_own = decode_input.reshape(n, width)
    group_rows = x_group.shape[0]
    rows_share = group_rows // lax.axis_size("grp")
    each = -(-(n + 1) // 16) * 16
    numbers = jnp.concatenate(
        [prompt_len // PAGE, prompt_len % PAGE, page_counts[:, 0], slot_target.reshape(-1)]
    ).astype(bf16)
    numbers = jnp.pad(numbers, (0, width - numbers.shape[0]))[None]
    payload = jnp.concatenate([dec_own, numbers, jnp.zeros((each - n - 1, width), bf16)], axis=0)
    members = lax.axis_size("grp")
    block = lax.dynamic_slice_in_dim(payload, col, share, 1).reshape(-1, LAT + ROPE)
    share_rows = lax.dynamic_slice_in_dim(x_group, grp_index * rows_share, rows_share, 0)
    share_place = seq_index * group_rows + grp_index * rows_share + jnp.arange(rows_share)
    own_place = (prompt_len[None, :] + jnp.arange(each // reqs)[:, None]).reshape(-1)
    block, fresh = prepare(
        rows_share,
        jnp.concatenate([share_rows, payload]),
        latent_proj,
        *turns(jnp.concatenate([share_place, own_place])),
        block,
    )
    blocks = gather_blocks(block, owners, members)
    shard_rows = blocks[:, :, :rows_share].reshape(-1, LAT + ROPE)
    dec_all = (
        blocks[:, :, rows_share:]
        .reshape(owners, members, each, share)
        .transpose(0, 2, 1, 3)
        .reshape(owners * each, width)
    )
    numbers = dec_all.reshape(owners, each, width)[:, n, : 2 * reqs + owners + owners * cap]
    ints = numbers.astype(jnp.int32)
    lens_all = ints[:, :reqs] * PAGE + ints[:, reqs : 2 * reqs]
    counts = lax.dynamic_slice_in_dim(ints, 2 * reqs + seq_index, 1, 1)
    targets = lax.dynamic_slice_in_dim(ints, 2 * reqs + owners + seq_index * cap, cap, 1)

    states = kda_state.astype(bf16).reshape((owners, reqs) + kda_state.shape[1:])
    states = lax.all_to_all(states, "seq", split_axis=0, concat_axis=0, tiled=True)

    position = seq_index * group_rows + jnp.arange(group_rows)
    dec_place = (lens_all[:, None, :] + jnp.arange(each // reqs)[None, :, None]).reshape(-1)
    queries, qc = make_queries(
        x_group,
        dec_all,
        owners,
        query_proj,
        key_expand,
        *turns(jnp.concatenate([position, dec_place])),
    )

    pages = latent_pages.reshape(owners, cap * PAGE, LAT + ROPE)
    token = (targets % MAXP)[..., None] * PAGE + jnp.arange(PAGE)
    holder = targets // MAXP
    length = jnp.sum(
        jnp.where(holder[..., None] == jnp.arange(reqs), lens_all[:, None, :], 0), axis=-1
    )
    live = (jnp.arange(cap)[None, :] < counts)[..., None] & (token < length[..., None])
    holders = jnp.where(live, holder[..., None], -1).reshape(owners, 1, cap * PAGE)
    sent = attend_pages(reqs, qc, pages, holders, value_expand)
    sent, shard_rows = lax.optimization_barrier((sent, shard_rows))
    came = lax.all_to_all(
        sent.reshape(owners, each, -1), "seq", split_axis=0, concat_axis=0, tiled=True
    )

    prefill_part = prefill_attend(
        seq_index, members, queries, shard_rows, key_expand, value_expand, mla_output
    )
    came, prefill_part = lax.optimization_barrier((came, prefill_part))
    attended = lax.psum_scatter(prefill_part, "grp", scatter_dimension=0, tiled=False)

    pieces = lax.axis_size("grp")
    own_query = lax.dynamic_index_in_dim(qc, seq_index, 0, keepdims=False)
    own_query = own_query.reshape(heads, each, LAT + ROPE)
    mla_parts = merge_parts(
        reqs, n, pieces, came, own_query, fresh, value_expand, mla_output
    )
    mla_total = sum_over_grp(mla_parts)
    kda_parts = delta_steps(
        steps,
        reqs,
        mla_total,
        payload,
        kda_inputs.transpose(1, 0, 2),
        kda_beta,
        decay_down,
        decay_up,
        gate_down,
        gate_up,
        jnp.repeat(jnp.exp(decay_log), DK)[None],
        states,
        kda_output,
    )
    kda_parts, attended = lax.optimization_barrier((kda_parts, attended))
    dec_share = lax.dynamic_slice_in_dim(payload, col, share, 1)
    decode_out = sum_over_grp(kda_parts, mla_total, dec_share)
    prefill_out = (
        lax.dynamic_slice_in_dim(x_group, col, share, 1).astype(f32) + attended.astype(f32)
    ).astype(bf16)
    return (prefill_out, decode_out[:n].reshape(steps, reqs, share))


def solution(mesh):
    in_specs = (
        P("seq", None),
        P(None, "seq", None),
        P("seq"),
        P("seq", None, None, None, None),
        P(None, "seq", None),
        P(None, "seq"),
        P(None, "grp", "seq", None),
        P(None, "grp"),
        P(),
        P(None, "grp"),
        P(None, "grp"),
        P("grp", None),
        P(None, None, "grp"),
        P(None, "grp"),
        P(),
        P(None, "grp"),
        P(),
        P(None, "grp"),
        P("grp"),
        P("grp", None),
    )
    out_specs = (P("seq", "grp"), P(None, "seq", "grp"))
    return jax.shard_map(shards, mesh=mesh, in_specs=in_specs, out_specs=out_specs, check_vma=False)
```
